128 devices in a mesh: lat: 8 (over y, core), lon: 16 (over x, z).
Axes of the slice: x: 4, y: 4, z: 4, core: 2. Of those that a mesh axis runs over, the one named last changes fastest.
Arguments:
- node_states: bfloat16 [65536, 512], P(('lat', 'lon')), may hold values from -6 to 6
- edge_states: bfloat16 [262144, 512], P(('lat', 'lon')), may hold values from -6 to 6
- senders: int32 [262144], P(('lat', 'lon')), may hold values from 0 to 767, as said below
- receivers: int32 [262144], P(('lat', 'lon')), may hold values from 0 to 511
- live_count: int32 [128], P(('lat', 'lon')), may hold values from 256 to 2048, as said below
- send_rows: int32 [128, 256], P(('lat', 'lon')), may hold values from 0 to 511
- node_cotangent: bfloat16 [65536, 512], P(('lat', 'lon')), may hold values from -6 to 6
- edge_inner: bfloat16 [1536, 512], replicated, may hold values from -0.15625 to 0.15625
- edge_inbias: float32 [512], replicated, may hold values from -3 to 3
- edge_outer: bfloat16 [512, 512], replicated, may hold values from -0.25 to 0.25
- edge_outbias: float32 [512], replicated, may hold values from -3 to 3
- edge_gain: float32 [512], replicated, may hold values from 0.1 to 1.9
- node_inner: bfloat16 [1024, 512], replicated, may hold values from -0.1875 to 0.1875
- node_inbias: float32 [512], replicated, may hold values from -3 to 3
- node_outer: bfloat16 [512, 512], replicated, may hold values from -0.25 to 0.25
- node_outbias: float32 [512], replicated, may hold values from -3 to 3
- node_gain: float32 [512], replicated, may hold values from 0.1 to 1.9
Outputs:
- new_nodes: bfloat16 [65536, 512], P(('lat', 'lon'))
- node_grad: bfloat16 [65536, 512], P(('lat', 'lon'))
- edge_grad: bfloat16 [262144, 512], P(('lat', 'lon'))
- edge_inner_grad: float32 [1536, 512], replicated
- edge_inbias_grad: float32 [512], replicated
- edge_outer_grad: float32 [512, 512], replicated
- edge_outbias_grad: float32 [512], replicated
- edge_gain_grad: float32 [512], replicated
- node_inner_grad: float32 [1024, 512], replicated
- node_inbias_grad: float32 [512], replicated
- node_outer_grad: float32 [512, 512], replicated
- node_outbias_grad: float32 [512], replicated
- node_gain_grad: float32 [512], replicated
The draws below stay inside these ranges and needn't reach their ends.
Inputs may be any that keep to these rules, and one draw needn't show every extreme that they name: `senders`: below 512 an edge's sender is a node of its own patch; 512 + n * 32 + s names the s-th row that its neighbour n sends to it. No edge names a neighbour beyond the first or last lat index. Both ends of the range occur. `live_count`: edge rows of a patch past this count are padding; some patch has all 2048 rows live. send_rows[p, n * 32 + s] is a node of patch p that it sends to its neighbour n; rows may repeat.
All inputs are finite; a program needn't handle non-finite values.
Results may differ from the reference program's by a relative error of at most 0.015.
Values may be sent and summed in bfloat16 or wider, within the bound.
A program may use at most 192 MiB of HBM per device.

```python
import jax
import jax.numpy as jnp
from jax import lax

D = 512
NODE_DEV = 512
E_DEV = 2048
SLOT = 32
PATCHES = 128
NODES = 65536
EDGES = 262144
PEER_SLOTS = 256
N_LAT = 8
N_LON = 16


def draw_senders(key, part):
    key = jax.random.fold_in(key, 11)
    subkeys = jax.random.split(key, 4)
    choose = jax.random.randint(subkeys[0], (EDGES,), 0, 4)
    local_pick = jax.random.randint(subkeys[1], (EDGES,), 0, NODE_DEV)
    neighbour = jax.random.randint(subkeys[2], (EDGES,), 0, 8)
    position = jnp.arange(EDGES, dtype=jnp.int32)
    lat_index = position // E_DEV // N_LON
    low_bad = jnp.logical_and(lat_index == 0, neighbour < 3)
    high_bad = jnp.logical_and(lat_index == N_LAT - 1, neighbour >= 5)
    neighbour = jnp.where(low_bad, neighbour + 5, neighbour)
    neighbour = jnp.where(high_bad, neighbour - 5, neighbour)
    remote_pick = NODE_DEV + neighbour * SLOT + jax.random.randint(subkeys[3], (EDGES,), 0, SLOT)
    picked = jnp.where(choose == 0, remote_pick, local_pick)
    picked = jnp.where(position == 0, 0, picked)
    picked = jnp.where(position == 1, NODE_DEV + PEER_SLOTS - 1, picked)
    return picked.astype(jnp.int32)


def draw_live_count(key, part):
    key = jax.random.fold_in(key, 23)
    subkeys = jax.random.split(key, 3)
    first = jax.random.randint(subkeys[0], (PATCHES,), 0, 65)
    second = jax.random.randint(subkeys[1], (PATCHES,), 0, 65)
    lowest = E_DEV // 8
    counts = lowest + (E_DEV - lowest) * first * second // 4096
    busiest = jax.random.randint(subkeys[2], (), 0, PATCHES)
    counts = jnp.where(jnp.arange(PATCHES, dtype=jnp.int32) == busiest, E_DEV, counts)
    return counts.astype(jnp.int32)


def set_ends(array, stream_key, smallest, largest):
    shape = array.shape
    spot = [jax.random.randint(jax.random.fold_in(stream_key, axis), (), 0, shape[axis]) for axis in range(len(shape))]
    array = array.at[tuple(spot)].set(smallest)
    longest = shape.index(max(shape))
    spot[longest] = (spot[longest] + 1) % shape[longest]
    return array.at[tuple(spot)].set(largest)


def block_levels(stream_key, dims, cuts, low, top_value):
    def one(dim, shards_of):
        steps = jax.random.uniform(jax.random.fold_in(jax.random.fold_in(stream_key, 6), dim), (shards_of,), jnp.float32, low / len(cuts), top_value / len(cuts))
        return jnp.repeat(jnp.exp(steps), dims[dim] // shards_of).reshape((-1,) + (1,) * (len(dims) - dim - 1))

    level = one(*cuts[0])
    for cut in cuts[1:]:
        level = level * one(*cut)
    return level


def gaussian(rng, shape, spread, bound, pieces=(), kind=jnp.bfloat16):
    level = block_levels(rng, shape, pieces, -0.22, 0.18) if pieces else 1.0
    values = jax.random.normal(rng, shape, jnp.float32) * spread * level
    return jnp.minimum(jnp.maximum(values, -bound), bound).astype(kind)


def setup_inputs(seed: int = 0) -> dict:
    arg_keys = jax.random.split(jax.random.key(seed), 18)
    return {
        "node_states": gaussian(arg_keys[0], (NODES, D), 1.0, 6.0, ((0, 128),)),
        "edge_states": gaussian(arg_keys[1], (EDGES, D), 1.0, 6.0, ((0, 128),)),
        "senders": draw_senders(jax.random.fold_in(arg_keys[17], 71), 0),
        "receivers": set_ends(jax.random.randint(arg_keys[3], (EDGES,), 0, NODE_DEV), jax.random.fold_in(arg_keys[3], 1), 0, NODE_DEV - 1).astype(jnp.int32),
        "live_count": draw_live_count(jax.random.fold_in(arg_keys[17], 71), 0),
        "send_rows": set_ends(jax.random.randint(arg_keys[5], (PATCHES, PEER_SLOTS), 0, NODE_DEV), jax.random.fold_in(arg_keys[5], 1), 0, NODE_DEV - 1).astype(jnp.int32),
        "node_cotangent": gaussian(arg_keys[6], (NODES, D), 1.0, 6.0, ((0, 128),)),
        "edge_inner": gaussian(arg_keys[7], (3 * D, D), (3 * D) ** -0.5, 0.15625),
        "edge_inbias": gaussian(arg_keys[8], (D,), 0.5, 3.0, (), jnp.float32),
        "edge_outer": gaussian(arg_keys[9], (D, D), D ** -0.5, 0.25),
        "edge_outbias": gaussian(arg_keys[10], (D,), 0.5, 3.0, (), jnp.float32),
        "edge_gain": jnp.clip(1.0 + 0.18 * jax.random.normal(arg_keys[11], (D,), jnp.float32), 0.1, 1.9),
        "node_inner": gaussian(arg_keys[12], (2 * D, D), (2 * D) ** -0.5, 0.1875),
        "node_inbias": gaussian(arg_keys[13], (D,), 0.5, 3.0, (), jnp.float32),
        "node_outer": gaussian(arg_keys[14], (D, D), D ** -0.5, 0.25),
        "node_outbias": gaussian(arg_keys[15], (D,), 0.5, 3.0, (), jnp.float32),
        "node_gain": jnp.clip(1.0 + 0.18 * jax.random.normal(arg_keys[16], (D,), jnp.float32), 0.1, 1.9),
    }


epsilon = 1e-05

def silu_slope(preact):
    sigmoid = jax.nn.sigmoid(preact)
    return sigmoid * (1.0 + preact * (1.0 - sigmoid))

def normalize(output):
    centered = output - lax.optimization_barrier(jnp.mean(output, axis=-1, keepdims=True))
    inv_scale = lax.rsqrt(lax.optimization_barrier(jnp.mean(centered * centered, axis=-1, keepdims=True)) + epsilon)
    return (centered * inv_scale, inv_scale)

def norm_back(scaled_grad, normed, inv_scale):
    mean_grad = lax.optimization_barrier(jnp.mean(scaled_grad, axis=-1, keepdims=True))
    mean_cross = lax.optimization_barrier(jnp.mean(scaled_grad * normed, axis=-1, keepdims=True))
    return inv_scale * (scaled_grad - mean_grad - normed * mean_cross)

def mlp_forward(inputs, weight_in, bias_in, weight_out, bias_out, gain_vec):
    preact = jnp.dot(inputs, weight_in, preferred_element_type=jnp.float32) + bias_in
    hidden = jax.nn.silu(preact).astype(jnp.bfloat16)
    output = jnp.dot(hidden, weight_out, preferred_element_type=jnp.float32) + bias_out
    normed, inv_scale = normalize(output)
    return (normed * gain_vec, (preact, hidden, normed, inv_scale))

def mlp_backward(inputs, saved_state, output_grad, weight_in, weight_out, gain_vec):
    preact, hidden, normed, inv_scale = saved_state
    gain_grad = lax.optimization_barrier(jnp.sum(output_grad * normed, axis=0))
    post_grad = norm_back(output_grad * gain_vec, normed, inv_scale)
    outbias_grad = lax.optimization_barrier(jnp.sum(post_grad, axis=0))
    post_round = post_grad.astype(jnp.bfloat16)
    outer_grad = jnp.dot(hidden.T, post_round, preferred_element_type=jnp.float32)
    hidden_grad = jnp.dot(post_round, weight_out.T, preferred_element_type=jnp.float32)
    pre_grad = hidden_grad * silu_slope(preact)
    inbias_grad = lax.optimization_barrier(jnp.sum(pre_grad, axis=0))
    pre_round = pre_grad.astype(jnp.bfloat16)
    inner_grad = jnp.dot(inputs.T, pre_round, preferred_element_type=jnp.float32)
    inputs_grad = jnp.dot(pre_round, weight_in.T, preferred_element_type=jnp.float32)
    return (inputs_grad, (inner_grad, inbias_grad, outer_grad, outbias_grad, gain_grad))

def patch_pass(own_nodes, own_edges, sender_feat, own_receivers, live_mask, own_cotangent, params):
    edge_inner, edge_inbias, edge_outer, edge_outbias, edge_gain, node_inner, node_inbias, node_outer, node_outbias, node_gain = params
    features = own_nodes.shape[1]
    node_count = own_nodes.shape[0]
    edge_in = jnp.concatenate([own_edges, sender_feat, own_nodes[own_receivers]], axis=1)
    edge_out, edge_saved = mlp_forward(edge_in, edge_inner, edge_inbias, edge_outer, edge_outbias, edge_gain)
    new_edges = (own_edges.astype(jnp.float32) + edge_out).astype(jnp.bfloat16)
    masked = jnp.where(live_mask[:, None], new_edges.astype(jnp.float32), jnp.float32(0.0))
    summed = jax.ops.segment_sum(masked, own_receivers, num_segments=node_count).astype(jnp.bfloat16)
    node_in = jnp.concatenate([own_nodes, summed], axis=1)
    node_out, node_saved = mlp_forward(node_in, node_inner, node_inbias, node_outer, node_outbias, node_gain)
    new_nodes = (own_nodes.astype(jnp.float32) + node_out).astype(jnp.bfloat16)
    cotangent = own_cotangent.astype(jnp.float32)
    node_in_grad, node_terms = mlp_backward(node_in, node_saved, cotangent, node_inner, node_outer, node_gain)
    edge_out_grad = jnp.where(live_mask[:, None], node_in_grad[:, features:][own_receivers], jnp.float32(0.0))
    edge_in_grad, edge_terms = mlp_backward(edge_in, edge_saved, edge_out_grad, edge_inner, edge_outer, edge_gain)
    edge_grad = (edge_out_grad + edge_in_grad[:, :features]).astype(jnp.bfloat16)
    receiver_part = jax.ops.segment_sum(edge_in_grad[:, 2 * features:], own_receivers, num_segments=node_count)
    local_grad = cotangent + node_in_grad[:, :features] + receiver_part
    sender_grad = edge_in_grad[:, features:2 * features]
    return (new_nodes, edge_grad, local_grad, sender_grad, edge_terms + node_terms)

def reference(node_states, edge_states, senders, receivers, live_count, send_rows, node_cotangent, edge_inner, edge_inbias, edge_outer, edge_outbias, edge_gain, node_inner, node_inbias, node_outer, node_outbias, node_gain):
    params = (edge_inner, edge_inbias, edge_outer, edge_outbias, edge_gain, node_inner, node_inbias, node_outer, node_outbias, node_gain)
    device_ids = jnp.arange(PATCHES, dtype=jnp.int32)
    local_ids = senders.reshape(PATCHES, E_DEV).astype(jnp.int32)
    slot_pos = jnp.maximum(local_ids - NODE_DEV, 0).astype(jnp.int32)
    neighbour = (slot_pos // SLOT).astype(jnp.int32)
    cell = (neighbour + (neighbour >= 4).astype(jnp.int32)).astype(jnp.int32)
    lat_own = (device_ids // N_LON).astype(jnp.int32)
    lon_own = (device_ids % N_LON).astype(jnp.int32)
    lat_peer = jnp.clip(lat_own[:, None] + cell // 3 - 1, 0, N_LAT - 1).astype(jnp.int32)
    lon_peer = ((lon_own[:, None] + cell % 3 - 1 + N_LON) % N_LON).astype(jnp.int32)
    source_patch = (lat_peer * N_LON + lon_peer).astype(jnp.int32)
    slot_column = ((7 - neighbour) * SLOT + slot_pos % SLOT).astype(jnp.int32)
    remote_rows = send_rows[source_patch, slot_column].astype(jnp.int32)
    global_rows = jnp.where(local_ids < NODE_DEV, device_ids[:, None] * NODE_DEV + local_ids, source_patch * NODE_DEV + remote_rows).astype(jnp.int32)
    features = node_states.shape[1]

    def one_patch(carry, inputs):
        grad_table, totals = carry
        device, rows_global, own_nodes, own_edges, own_receivers, own_live, own_cotangent = inputs
        sender_feat = node_states[rows_global]
        live_mask = jnp.arange(E_DEV, dtype=jnp.int32) < own_live
        new_rows, edge_rows, local_grad, sender_grad, grads = patch_pass(own_nodes, own_edges, sender_feat, own_receivers, live_mask, own_cotangent, params)
        grad_table = grad_table.at[rows_global].add(sender_grad)
        node_rows = (device * NODE_DEV + jnp.arange(NODE_DEV, dtype=jnp.int32)).astype(jnp.int32)
        grad_table = grad_table.at[node_rows].add(local_grad)
        totals = jax.tree.map(jnp.add, totals, grads)
        return ((grad_table, totals), (new_rows, edge_rows))
    start_table = jnp.zeros((NODES, features), jnp.float32)
    start_totals = tuple((jnp.zeros(weight.shape, jnp.float32) for weight in params))
    inputs = (device_ids, global_rows, node_states.reshape(PATCHES, NODE_DEV, features), edge_states.reshape(PATCHES, E_DEV, features), receivers.reshape(PATCHES, E_DEV).astype(jnp.int32), live_count.astype(jnp.int32), node_cotangent.reshape(PATCHES, NODE_DEV, features))
    (grad_table, totals), (new_rows, edge_rows) = lax.scan(one_patch, (start_table, start_totals), inputs)
    new_nodes = new_rows.reshape(NODES, features)
    edge_grad = edge_rows.reshape(EDGES, features)
    node_grad = grad_table.astype(jnp.bfloat16)
    return (new_nodes, node_grad, edge_grad, totals[0], totals[1], totals[2], totals[3], totals[4], totals[5], totals[6], totals[7], totals[8], totals[9])
```

```python
import functools

import jax
import jax.numpy as jnp
from jax import lax
from jax.experimental import pallas as pl
from jax.experimental.pallas import tpu as pltpu
from jax.sharding import PartitionSpec as P

MESH = pl.DeviceIdType.MESH
F32 = jnp.float32
BF16 = jnp.bfloat16
I32 = jnp.int32
epsilon = 1e-05

D = 512
NODE = 512
EDGE = 2048
SLOT = 32
PEER = 256
TABLE = NODE + PEER
WIDE = TABLE + NODE
CHUNK = 512
STEPS = EDGE // CHUNK
LANE = 128
N_LAT = 8
N_LON = 16
OFFSETS = ((-1, -1), (-1, 0), (-1, 1), (0, -1), (0, 1), (1, -1), (1, 0), (1, 1))


def dot(a, b):
    return jnp.dot(a, b, preferred_element_type=F32)


def dot_rt(a, b):
    return lax.dot_general(a, b, (((1,), (1,)), ((), ())), preferred_element_type=F32)


def dot_lt(a, b):
    return lax.dot_general(a, b, (((0,), (0,)), ((), ())), preferred_element_type=F32)


def row_mean(x):
    return jnp.sum(x, axis=-1, keepdims=True) * (1.0 / D)


def col_sum(x):
    return jnp.sum(x, axis=0, keepdims=True)


def silu_parts(z):
    sig = 0.5 + 0.5 * jnp.tanh(0.5 * z)
    h = z * sig
    return h, sig + h * (1.0 - sig)


def normalize(post):
    centered = post - row_mean(post)
    scale = lax.rsqrt(row_mean(centered * centered) + epsilon)
    return centered * scale, scale


def norm_back(t, normed, scale):
    return scale * (t - row_mean(t) - normed * row_mean(t * normed))


def column_of(row):
    return jnp.transpose(jnp.broadcast_to(row.astype(F32), (LANE, LANE))).astype(I32)


def lanes(base):
    return lax.broadcasted_iota(I32, (LANE, LANE), 1) + base


def hot(mask):
    return jnp.where(mask, 1.0, 0.0).astype(BF16)


class Place:
    def __init__(self):
        self.lat = lax.axis_index("lat")
        self.lon = lax.axis_index("lon")
        self.core = lax.rem(self.lat, 2)
        self.y = lax.div(self.lat, 2)
        self.x = lax.div(self.lon, 4)
        self.z = lax.rem(self.lon, 4)

    def neighbour(self, n):
        dlat, dlon = OFFSETS[n]
        return (
            lax.rem(self.lat + (dlat + N_LAT), N_LAT),
            lax.rem(self.lon + (dlon + N_LON), N_LON),
        )

    def twin(self):
        return (self.y * 2 + (1 - self.core), self.lon)

    def index(self, axis):
        is_x = lax.div((2 - axis) * (1 - axis), 2)
        is_y = axis * (2 - axis)
        is_z = lax.div(axis * (axis - 1), 2)
        return self.x * is_x + self.y * is_y + self.z * is_z

    def shifted(self, axis, d):
        is_x = lax.div((2 - axis) * (1 - axis), 2)
        is_y = axis * (2 - axis)
        is_z = lax.div(axis * (axis - 1), 2)
        x = lax.rem(self.x + d * is_x, 4)
        y = lax.rem(self.y + d * is_y, 4)
        z = lax.rem(self.z + d * is_z, 4)
        return (y * 2 + self.core, x * 4 + z)

    def axis(self, b, level):
        return lax.rem(self.core + (b + level), 3)


class Reduce:
    def __init__(self, place, nb, gb, rc, s0, r1, s1, r2, s2, r3, fin, send, recv):
        self.p, self.nb = place, nb
        self.gb, self.rc, self.s0, self.r1, self.s1 = gb, rc, s0, r1, s1
        self.r2, self.s2, self.r3, self.fin = r2, s2, r3, fin
        self.send, self.recv = send, recv
        self.copies = {}

    def pack(self, j, val):
        for b in range(4):
            part = val[:, b * LANE : (b + 1) * LANE].astype(BF16)
            self.gb[:, b, :, :, j] = part.reshape(2, 4, 4, 16, LANE)

    def copy(self, step, k, src, dst, device):
        at = 1 + (step - 1) * 12 + k if 1 <= step <= 5 else (0 if step == 0 else 61)
        c = pltpu.make_async_remote_copy(
            src_ref=src,
            dst_ref=dst,
            send_sem=self.send.at[at],
            recv_sem=self.recv.at[at],
            device_id=device,
            device_id_type=MESH,
        )
        c.start()
        self.copies.setdefault(step, []).append(c)

    def wait(self, step):
        for c in self.copies[step]:
            c.wait_recv()

    def spread(self, step, level, src, dst):
        for b in range(4):
            axis = self.p.axis(b, level)
            for d in (2, 1, 3):
                there = lax.rem(self.p.index(axis) + d, 4)
                self.copy(
                    step, b * 3 + d - 1, src(b, there), dst(b, d), self.p.shifted(axis, d)
                )

    def step(self, k):
        h = self.p.core
        own = [self.p.index(self.p.axis(b, 0)) for b in range(4)]
        own2 = [self.p.index(self.p.axis(b, 1)) for b in range(4)]
        if k == 0:
            self.copy(0, 0, self.gb.at[1 - h], self.rc, self.p.twin())
        elif k == 1:
            self.wait(0)
            for b in range(4):
                mine = self.gb[h, b].astype(F32)
                self.s0[b] = (mine + self.rc[b].astype(F32)).astype(BF16)
            self.spread(1, 0, lambda b, i: self.s0.at[b, i], lambda b, d: self.r1.at[b, d - 1])
        elif k == 2:
            self.wait(1)
            for b in range(4):
                total = self.s0[b, own[b]].astype(F32)
                for d in range(3):
                    total += self.r1[b, d].astype(F32)
                self.s1[b] = total.astype(BF16)
            self.spread(2, 1, lambda b, i: self.s1.at[b, i], lambda b, d: self.r2.at[b, d - 1])
        elif k == 3:
            self.wait(2)
            for b in range(4):
                total = self.s1[b, own2[b]].astype(F32)
                for d in range(3):
                    total += self.r2[b, d].astype(F32)
                self.s2[b] = total.astype(BF16)
            self.spread(3, 2, lambda b, i: self.s2.at[b], lambda b, d: self.r3.at[b, d - 1])
        elif k == 4:
            self.wait(3)
            for b in range(4):
                near = self.s2[b].astype(F32) + self.r3[b, 1].astype(F32)
                far = self.r3[b, 0].astype(F32) + self.r3[b, 2].astype(F32)
                self.fin[h, b, own[b], own2[b]] = (near + far).astype(BF16)

            def piece(b, _):
                return self.fin.at[h, b, own[b], own2[b]]

            self.spread(4, 1, piece, piece)
        elif k == 5:
            self.wait(4)

            def piece(b, _):
                return self.fin.at[h, b, own[b]]

            self.spread(5, 0, piece, piece)
        elif k == 6:
            self.wait(5)
            self.copy(6, 0, self.fin.at[h], self.fin.at[h], self.p.twin())
        elif k == 7:
            self.wait(6)

    def drain(self):
        for group in self.copies.values():
            for c in group:
                c.wait_send()


class Vectors:
    def __init__(self, place, val, slots, send, recv):
        self.p, self.val, self.slots, self.send, self.recv = place, val, slots, send, recv
        self.copies = []

    def start(self, k):
        axis = k - 1
        hops = ((0, self.p.twin()),) if k == 0 else tuple(
            (d, self.p.shifted(jnp.int32(axis), d)) for d in (1, 2, 3)
        )
        for d, device in hops:
            at = 0 if k == 0 else 3 * (k - 1) + d
            c = pltpu.make_async_remote_copy(
                src_ref=self.val.at[k],
                dst_ref=self.slots.at[at],
                send_sem=self.send.at[at],
                recv_sem=self.recv.at[at],
                device_id=device,
                device_id_type=MESH,
            )
            c.start()
            self.copies.append((k, c))

    def finish(self, k):
        for j, c in self.copies:
            if j == k:
                c.wait_recv()
        if k == 0:
            self.val[1] = self.val[0] + self.slots[0]
        else:
            at = 3 * (k - 1)
            near = self.val[k] + self.slots[at + 2]
            far = self.slots[at + 1] + self.slots[at + 3]
            self.val[k + 1] = near + far

    def drain(self):
        for _, c in self.copies:
            c.wait_send()


def layer(
    nodes_h, edges_h, senders, receivers, live, send_rows, cot_h,
    wei_h, eib, weo_h, eob, egain, wni_h, nib, wno_h, nob, ngain,
    new_nodes_h, node_grad_h, edge_grad_h, fin_a_h, fin_b_h, fin_c_h, vec_h,
    nodes, edges, cot, wei, weo, wni, wno,
    ohs, oht, ohr, pre, hid, normed, scale, gath, prnd,
    table, grad_rows, zb, halo_out, halo_in, back_out, back_in, sendt,
    new_nodes, node_base, node_grad, summed, acc,
    bufs_a, bufs_b, bufs_c, vec, vec_slots,
    in_sem, out_sem, halo_send, halo_recv, sems_a, sems_b, sems_c, sems_v,
):
    place = Place()
    staging = normed
    prd = ohs.at[:, 0:D]

    def load(k, src, dst):
        c = pltpu.make_async_copy(src, dst, in_sem.at[k])
        c.start()
        return c

    def store(k, src, dst):
        c = pltpu.make_async_copy(src, dst, out_sem.at[k])
        c.start()
        return c

    c_nodes = load(0, nodes_h, nodes)
    c_wei = load(1, wei_h, wei)
    c_edges = load(2, edges_h, edges)
    c_weo = load(3, weo_h, weo)
    c_wni = load(4, wni_h, wni)
    c_wno = load(5, wno_h, wno)
    c_cot = load(6, cot_h, cot)

    barrier = pltpu.get_barrier_semaphore()
    partners = [place.neighbour(n) for n in range(8)] + [place.twin()]
    for axis in range(3):
        for d in (1, 2, 3):
            partners.append(place.shifted(jnp.int32(axis), d))
    for device in partners:
        pl.semaphore_signal(barrier, inc=1, device_id=device, device_id_type=MESH)

    red_a = Reduce(place, 3, *bufs_a, *sems_a)
    red_b = Reduce(place, 2, *bufs_b, *sems_b)
    red_c = Reduce(place, 2, *bufs_c, *sems_c)
    red_v = Vectors(place, vec, vec_slots, *sems_v)

    c_nodes.wait()
    picks = []
    for k in range(2):
        col = column_of(send_rows[:, k * LANE : (k + 1) * LANE])
        picks.append(jnp.concatenate([hot(col == lanes(j * LANE)) for j in range(4)], axis=1))
    listed = dot(jnp.concatenate(picks, axis=0), nodes[...]).astype(BF16)
    halo_out[...] = listed.reshape(8, SLOT, D)
    pl.semaphore_wait(barrier, len(partners))

    def exchange(src, dst, base):
        copies = []
        for n in range(8):
            c = pltpu.make_async_remote_copy(
                src_ref=src.at[n],
                dst_ref=dst.at[7 - n],
                send_sem=halo_send.at[base + n],
                recv_sem=halo_recv.at[base + 7 - n],
                device_id=place.neighbour(n),
                device_id_type=MESH,
            )
            c.start()
            copies.append(c)
        return copies

    halo = exchange(halo_out, halo_in, 0)

    rowi = lax.broadcasted_iota(I32, (NODE, LANE), 0)
    for k in range(2):
        row = send_rows[:, k * LANE : (k + 1) * LANE]
        sendt[:, k * LANE : (k + 1) * LANE] = hot(rowi == row)
    c_wei.wait()
    table[0:NODE, :] = dot(nodes[...], wei[D : 2 * D, :]).astype(BF16)
    table[TABLE:WIDE, :] = dot(nodes[...], wei[2 * D : 3 * D, :]).astype(BF16)
    c_edges.wait()

    def early(c, _):
        base = pl.multiple_of(c * CHUNK, CHUNK)
        rows = pl.ds(base, CHUNK)
        pre[rows, :] = dot(edges[rows, :], wei[0:D, :]) + eib[...]
        for j in range(CHUNK // LANE):
            s_row = senders[pl.ds(c * (CHUNK // LANE) + j, 1), :]
            r_row = receivers[pl.ds(c * (CHUNK // LANE) + j, 1), :]
            s_col, r_col = column_of(s_row), column_of(r_row)
            here = pl.ds(pl.multiple_of(base + j * LANE, LANE), LANE)
            for k in range(TABLE // LANE):
                ohs[here, k * LANE : (k + 1) * LANE] = hot(s_col == lanes(k * LANE))
            for k in range(NODE // LANE):
                ohr[here, k * LANE : (k + 1) * LANE] = hot(r_col == lanes(k * LANE))
            ids = lax.broadcasted_iota(I32, (TABLE, LANE), 0)
            oht[0:TABLE, here] = hot(ids == s_row)
            oht[TABLE:WIDE, here] = hot(rowi == r_row)
        return 0

    lax.fori_loop(0, STEPS, early, 0)

    for c in halo:
        c.wait_recv()
    incoming = halo_in[...].reshape(PEER, D)
    table[NODE:TABLE, :] = dot(incoming, wei[D : 2 * D, :]).astype(BF16)
    c_weo.wait()

    def is_live(base):
        return lax.broadcasted_iota(I32, (CHUNK, D), 0) < live[0] - base

    def forward(c, _):
        base = pl.multiple_of(c * CHUNK, CHUNK)
        rows = pl.ds(base, CHUNK)
        z = pre[rows, :] + dot(ohs[rows, :], table[0:TABLE, :])
        z = z + dot(ohr[rows, :], table[TABLE:WIDE, :])
        h, slope = silu_parts(z)
        hid[rows, :] = h.astype(BF16)
        pre[rows, :] = slope
        post = dot(hid[rows, :], weo[...]) + eob[...]
        unit, inv = normalize(post)
        normed[rows, :] = unit.astype(BF16)
        scale[rows, :] = inv
        new = edges[rows, :].astype(F32) + unit * egain[...]
        gath[rows, :] = jnp.where(is_live(base), new, 0.0).astype(BF16)
        return 0

    lax.fori_loop(0, STEPS, forward, 0)
    summed[...] = dot(oht[TABLE:WIDE, :], gath[...]).astype(BF16)

    c_wni.wait()
    c_wno.wait()
    c_cot.wait()
    z = dot(nodes[...], wni[0:D, :]) + dot(summed[...], wni[D : 2 * D, :]) + nib[...]
    h, slope = silu_parts(z)
    h = h.astype(BF16)
    unit, inv = normalize(dot(h, wno[...]) + nob[...])
    new_nodes[...] = (nodes[...].astype(F32) + unit * ngain[...]).astype(BF16)
    s_nodes = store(0, new_nodes, new_nodes_h)
    cotangent = cot[...].astype(F32)
    vec[0, 5:6, :] = col_sum(cotangent * unit)
    post_grad = norm_back(cotangent * ngain[...], unit, inv)
    vec[0, 4:5, :] = col_sum(post_grad)
    post_round = post_grad.astype(BF16)
    pre_grad = dot_rt(post_round, wno[...]) * slope
    vec[0, 3:4, :] = col_sum(pre_grad)
    pre_round = pre_grad.astype(BF16)
    grad_rows[...] = dot_rt(pre_round, wni[D : 2 * D, :]).astype(BF16)
    red_a.pack(2, dot_lt(h, post_round))
    red_a.pack(0, dot_lt(nodes[...], pre_round))
    red_a.pack(1, dot_lt(summed[...], pre_round))
    red_a.step(0)
    node_base[...] = cotangent + dot_rt(pre_round, wni[0:D, :])

    acc[...] = jnp.zeros_like(acc)

    def backward(c, _):
        base = pl.multiple_of(c * CHUNK, CHUNK)
        rows = pl.ds(base, CHUNK)
        g = jnp.where(is_live(base), dot(ohr[rows, :], grad_rows[...]), 0.0)
        gath[rows, :] = g.astype(BF16)
        unit = normed[rows, :].astype(F32)
        acc[2:3, :] += col_sum(g * unit)
        post_grad = norm_back(g * egain[...], unit, scale[rows, :])
        acc[1:2, :] += col_sum(post_grad)
        prnd[rows, :] = post_grad.astype(BF16)
        pre_grad = dot_rt(prnd[rows, :], weo[...]) * pre[rows, :]
        acc[0:1, :] += col_sum(pre_grad)
        prd[rows, :] = pre_grad.astype(BF16)
        return 0

    for c in range(STEPS):
        backward(c, 0)
        red_a.step(c + 1)
    vec[0, 0:3, :] = acc[0:3, :]
    vec[0, 6:8, :] = jnp.zeros((2, D), F32)
    red_v.start(0)

    red_b.pack(0, dot_lt(edges[...], prd[...]))
    red_b.pack(1, dot_lt(hid[...], prnd[...]))
    red_b.step(0)
    red_a.step(5)
    red_v.finish(0)
    red_v.start(1)
    for j in range(0, WIDE, 256):
        zb[j : j + 256, :] = dot(oht[j : j + 256, :], prd[...]).astype(BF16)
    red_b.step(1)
    red_c.pack(0, dot_lt(nodes[...], zb[0:NODE, :]) + dot_lt(incoming, zb[NODE:TABLE, :]))
    red_c.pack(1, dot_lt(nodes[...], zb[TABLE:WIDE, :]))
    red_c.step(0)
    red_a.step(6)
    red_v.finish(1)
    red_v.start(2)

    back = dot_rt(zb[NODE:TABLE, :], wei[D : 2 * D, :]).astype(BF16)
    back_out[...] = back.reshape(8, SLOT, D)
    returning = exchange(back_out, back_in, 8)
    red_b.step(2)
    node_base[...] += dot_rt(zb[0:NODE, :], wei[D : 2 * D, :])
    node_base[...] += dot_rt(zb[TABLE:WIDE, :], wei[2 * D : 3 * D, :])
    red_c.step(1)
    red_v.finish(2)
    red_v.start(3)

    stores = []

    def edge_out(c):
        rows = pl.ds(c * CHUNK, CHUNK)
        grad = dot_rt(prd[rows, :], wei[0:D, :])
        staging[rows, :] = (gath[rows, :].astype(F32) + grad).astype(BF16)
        stores.append(store(2 + c, staging.at[rows], edge_grad_h.at[rows]))

    edge_out(0)
    red_b.step(3)
    edge_out(1)
    red_c.step(2)
    red_b.step(4)
    edge_out(2)
    red_c.step(3)
    edge_out(3)
    red_b.step(5)
    for c in returning:
        c.wait_recv()
    owned = dot(sendt[...], back_in[...].reshape(PEER, D))
    node_grad[...] = (node_base[...] + owned).astype(BF16)
    stores.append(store(1, node_grad, node_grad_h))
    red_v.finish(3)
    stores.append(store(6, vec.at[4], vec_h))
    red_a.step(7)
    stores.append(store(7, red_a.fin, fin_a_h))
    red_c.step(4)
    red_b.step(6)
    red_c.step(5)
    red_b.step(7)
    stores.append(store(8, red_b.fin, fin_b_h))
    red_c.step(6)
    red_c.step(7)
    stores.append(store(9, red_c.fin, fin_c_h))
    for c in halo + returning:
        c.wait_send()
    for red in (red_a, red_b, red_c, red_v):
        red.drain()
    s_nodes.wait()
    for c in stores:
        c.wait()


def fin_shape(nb):
    return (2, 4, 4, 4, nb, 16, LANE)


def reduce_bufs(nb):
    tile = (nb, 16, LANE)
    return (
        pltpu.VMEM(fin_shape(nb), BF16),
        pltpu.VMEM((4, 4, 4) + tile, BF16),
        pltpu.VMEM((4, 4, 4) + tile, BF16),
        pltpu.VMEM((4, 3, 4) + tile, BF16),
        pltpu.VMEM((4, 4) + tile, BF16),
        pltpu.VMEM((4, 3) + tile, BF16),
        pltpu.VMEM((4,) + tile, BF16),
        pltpu.VMEM((4, 3) + tile, BF16),
        pltpu.VMEM(fin_shape(nb), BF16),
    )


def sem_pair(n):
    return (pltpu.SemaphoreType.DMA((n,)), pltpu.SemaphoreType.DMA((n,)))


def widen(fa, fb, fc, vec, edge_inner, edge_outer, node_inner, node_outer, *vecs):
    def put(src, j, out, k):
        for b in range(4):
            tile = src[0, b, 0, :, j].reshape(64, LANE).astype(F32)
            out[k, 0, :, b * LANE : (b + 1) * LANE] = tile

    put(fa, 0, node_inner, 0)
    put(fa, 1, node_inner, 1)
    put(fa, 2, node_outer, 0)
    put(fb, 0, edge_inner, 0)
    put(fb, 1, edge_outer, 0)
    put(fc, 0, edge_inner, 1)
    put(fc, 1, edge_inner, 2)
    for k in range(6):
        vecs[k][...] = vec[k : k + 1, :]


def unpack(fa, fb, fc, vec):
    def fin_spec(nb):
        return pl.BlockSpec((1, 4, 1, 4, nb, 16, LANE), lambda h, i: (h, 0, i, 0, 0, 0, 0))

    def out_spec(nb):
        return pl.BlockSpec((nb, 1, 64, D), lambda h, i: (0, h * 4 + i, 0, 0))

    counts = (3, 1, 2, 1)
    outs = pl.pallas_call(
        widen,
        grid=(2, 4),
        out_shape=[jax.ShapeDtypeStruct((n, 8, 64, D), F32) for n in counts]
        + [jax.ShapeDtypeStruct((1, D), F32)] * 6,
        in_specs=[fin_spec(3), fin_spec(2), fin_spec(2), pl.BlockSpec((8, D), lambda h, i: (0, 0))],
        out_specs=[out_spec(n) for n in counts]
        + [pl.BlockSpec((1, D), lambda h, i: (0, 0))] * 6,
        name="widen",
    )(fa, fb, fc, vec)
    mats = [o.reshape(n * D, D) for o, n in zip(outs, counts)]
    return mats, [v.reshape(D) for v in outs[4:]]


def body(
    node_states, edge_states, senders, receivers, live_count, send_rows, node_cotangent,
    edge_inner, edge_inbias, edge_outer, edge_outbias, edge_gain,
    node_inner, node_inbias, node_outer, node_outbias, node_gain,
):
    hbm = pl.BlockSpec(memory_space=pl.ANY)
    vm = pl.BlockSpec(memory_space=pltpu.VMEM)
    sm = pl.BlockSpec(memory_space=pltpu.SMEM)

    def row(v):
        return v.reshape(1, D)

    def v(shape, dtype=BF16):
        return pltpu.VMEM(shape, dtype)

    outs = pl.pallas_call(
        layer,
        out_shape=[
            jax.ShapeDtypeStruct((NODE, D), BF16),
            jax.ShapeDtypeStruct((NODE, D), BF16),
            jax.ShapeDtypeStruct((EDGE, D), BF16),
            jax.ShapeDtypeStruct(fin_shape(3), BF16),
            jax.ShapeDtypeStruct(fin_shape(2), BF16),
            jax.ShapeDtypeStruct(fin_shape(2), BF16),
            jax.ShapeDtypeStruct((8, D), F32),
        ],
        in_specs=[
            hbm, hbm, vm, vm, sm, vm, hbm,
            hbm, vm, hbm, vm, vm, hbm, vm, hbm, vm, vm,
        ],
        out_specs=[hbm] * 7,
        scratch_shapes=[
            v((NODE, D)), v((EDGE, D)), v((NODE, D)),
            v((3 * D, D)), v((D, D)), v((2 * D, D)), v((D, D)),
            v((EDGE, TABLE)), v((WIDE, EDGE)), v((EDGE, NODE)),
            v((EDGE, D), F32), v((EDGE, D)), v((EDGE, D)), v((EDGE, 1), F32),
            v((EDGE, D)), v((EDGE, D)),
            v((WIDE, D)), v((NODE, D)), v((WIDE, D)),
            v((8, SLOT, D)), v((8, SLOT, D)), v((8, SLOT, D)), v((8, SLOT, D)),
            v((NODE, PEER)),
            v((NODE, D)), v((NODE, D), F32), v((NODE, D)), v((NODE, D)), v((8, D), F32),
            reduce_bufs(3), reduce_bufs(2), reduce_bufs(2),
            v((5, 8, D), F32), v((10, 8, D), F32),
            pltpu.SemaphoreType.DMA((7,)), pltpu.SemaphoreType.DMA((10,)),
            pltpu.SemaphoreType.DMA((16,)), pltpu.SemaphoreType.DMA((16,)),
            sem_pair(62), sem_pair(62), sem_pair(62), sem_pair(10),
        ],
        compiler_params=pltpu.CompilerParams(
            collective_id=0, has_side_effects=True, vmem_limit_bytes=63 * 2**20
        ),
        name="layer",
    )(
        node_states, edge_states, senders.reshape(16, LANE), receivers.reshape(16, LANE),
        live_count, send_rows, node_cotangent,
        edge_inner, row(edge_inbias), edge_outer, row(edge_outbias), row(edge_gain),
        node_inner, row(node_inbias), node_outer, row(node_outbias), row(node_gain),
    )
    new_nodes, node_grad, edge_grad, fa, fb, fc, vec = outs
    mats, vecs = unpack(fa, fb, fc, vec)
    return (
        new_nodes, node_grad, edge_grad,
        mats[0], vecs[0], mats[1], vecs[1], vecs[2],
        mats[2], vecs[3], mats[3], vecs[4], vecs[5],
    )


def solution(mesh):
    nodes = P(("lat", "lon"), None)
    flat = P(("lat", "lon"))
    return jax.shard_map(
        body,
        mesh=mesh,
        in_specs=(nodes, nodes, flat, flat, flat, nodes, nodes) + (P(),) * 10,
        out_specs=(nodes, nodes, nodes) + (P(),) * 10,
        check_vma=False,
    )
```

```python
import functools

import jax
import jax.numpy as jnp
from jax import lax
from jax.experimental import pallas as pl
from jax.experimental.pallas import tpu as pltpu
from jax.sharding import PartitionSpec as P

MESH = pl.DeviceIdType.MESH
F32 = jnp.float32
BF16 = jnp.bfloat16
I32 = jnp.int32
epsilon = 1e-05

D = 512
NODE = 512
EDGE = 2048
SLOT = 32
PEER = 256
TABLE = NODE + PEER
WIDE = TABLE + NODE
CHUNK = 512
STEPS = EDGE // CHUNK
PART = 256
PARTS = EDGE // PART
SUB = 32
SUBS = PART // SUB
LANE = 128
N_LAT = 8
N_LON = 16
OFFSETS = ((-1, -1), (-1, 0), (-1, 1), (0, -1), (0, 1), (1, -1), (1, 0), (1, 1))


def dot(a, b):
    return jnp.dot(a, b, preferred_element_type=F32)


def dot_rt(a, b):
    return lax.dot_general(a, b, (((1,), (1,)), ((), ())), preferred_element_type=F32)


def dot_lt(a, b):
    return lax.dot_general(a, b, (((0,), (0,)), ((), ())), preferred_element_type=F32)


def row_mean(x):
    return jnp.sum(x, axis=-1, keepdims=True) * (1.0 / D)


def col_sum(x):
    return jnp.sum(x, axis=0, keepdims=True)


def silu_parts(z):
    sig = 0.5 + 0.5 * jnp.tanh(0.5 * z)
    h = z * sig
    return h, sig + h * (1.0 - sig)


def normalize(post):
    centered = post - row_mean(post)
    scale = lax.rsqrt(row_mean(centered * centered) + epsilon)
    return centered * scale, scale


def norm_back(t, normed, scale):
    return scale * (t - row_mean(t) - normed * row_mean(t * normed))


def column_of(row):
    return jnp.transpose(jnp.broadcast_to(row.astype(F32), (LANE, LANE))).astype(I32)


def lanes(base):
    return lax.broadcasted_iota(I32, (LANE, LANE), 1) + base


def hot(mask):
    return jnp.where(mask, 1.0, 0.0).astype(BF16)


class Place:
    def __init__(self):
        self.lat = lax.axis_index("lat")
        self.lon = lax.axis_index("lon")
        self.core = lax.rem(self.lat, 2)
        self.y = lax.div(self.lat, 2)
        self.x = lax.div(self.lon, 4)
        self.z = lax.rem(self.lon, 4)

    def neighbour(self, n):
        dlat, dlon = OFFSETS[n]
        return (
            lax.rem(self.lat + (dlat + N_LAT), N_LAT),
            lax.rem(self.lon + (dlon + N_LON), N_LON),
        )

    def twin(self):
        return (self.y * 2 + (1 - self.core), self.lon)

    def index(self, axis):
        is_x = lax.div((2 - axis) * (1 - axis), 2)
        is_y = axis * (2 - axis)
        is_z = lax.div(axis * (axis - 1), 2)
        return self.x * is_x + self.y * is_y + self.z * is_z

    def shifted(self, axis, d):
        is_x = lax.div((2 - axis) * (1 - axis), 2)
        is_y = axis * (2 - axis)
        is_z = lax.div(axis * (axis - 1), 2)
        x = lax.rem(self.x + d * is_x, 4)
        y = lax.rem(self.y + d * is_y, 4)
        z = lax.rem(self.z + d * is_z, 4)
        return (y * 2 + self.core, x * 4 + z)

    def axis(self, b, level):
        return lax.rem(self.core + (b + level), 3)


class Reduce:
    def __init__(self, place, streams, gb, rc, s0, r1, s1, r2, s2, r3, fin, send, recv):
        self.p, self.streams = place, streams
        self.gb, self.rc, self.s0, self.r1, self.s1 = gb, rc, s0, r1, s1
        self.r2, self.s2, self.r3, self.fin = r2, s2, r3, fin
        self.send, self.recv = send, recv
        self.copies = {}

    def pack(self, j, val):
        width = val.shape[1]
        self.gb[:, j] = val.astype(BF16).reshape(2, 4, 4, 16, width)

    def copy(self, step, k, src, dst, device):
        at = 1 + (step - 1) * 9 + k if 1 <= step <= 5 else (0 if step == 0 else 46)
        c = pltpu.make_async_remote_copy(
            src_ref=src,
            dst_ref=dst,
            send_sem=self.send.at[at],
            recv_sem=self.recv.at[at],
            device_id=device,
            device_id_type=MESH,
        )
        c.start()
        self.copies.setdefault(step, []).append(c)

    def wait(self, step):
        for c in self.copies[step]:
            c.wait_recv()

    def spread(self, step, level, src, dst):
        for n, part in enumerate(self.streams):
            axis = self.p.axis(n, level)
            for d in (2, 1, 3):
                there = lax.rem(self.p.index(axis) + d, 4)
                self.copy(
                    step, n * 3 + d - 1, src(n, part, there), dst(n, part, d), self.p.shifted(axis, d)
                )

    def step(self, k):
        h = self.p.core
        count = len(self.streams)
        own = [self.p.index(self.p.axis(n, 0)) for n in range(count)]
        own2 = [self.p.index(self.p.axis(n, 1)) for n in range(count)]
        if k == 0:
            self.copy(0, 0, self.gb.at[1 - h], self.rc, self.p.twin())
        elif k == 1:
            self.wait(0)
            for part in self.streams:
                mine = self.gb[h, part].astype(F32)
                self.s0[part] = (mine + self.rc[part].astype(F32)).astype(BF16)
            self.spread(
                1, 0, lambda n, part, i: self.s0.at[part, i], lambda n, part, d: self.r1.at[d - 1, part]
            )
        elif k == 2:
            self.wait(1)
            for n, part in enumerate(self.streams):
                total = self.s0[part, own[n]].astype(F32)
                for d in range(3):
                    total += self.r1[d, part].astype(F32)
                self.s1[part] = total.astype(BF16)
            self.spread(
                2, 1, lambda n, part, i: self.s1.at[part, i], lambda n, part, d: self.r2.at[d - 1, part]
            )
        elif k == 3:
            self.wait(2)
            for n, part in enumerate(self.streams):
                total = self.s1[part, own2[n]].astype(F32)
                for d in range(3):
                    total += self.r2[d, part].astype(F32)
                self.s2[part] = total.astype(BF16)
            self.spread(
                3, 2, lambda n, part, i: self.s2.at[part], lambda n, part, d: self.r3.at[d - 1, part]
            )
        elif k == 4:
            self.wait(3)
            for n, part in enumerate(self.streams):
                near = self.s2[part].astype(F32) + self.r3[1, part].astype(F32)
                far = self.r3[0, part].astype(F32) + self.r3[2, part].astype(F32)
                self.fin[h, part, own[n], own2[n]] = (near + far).astype(BF16)

            def piece(n, part, _):
                return self.fin.at[h, part, own[n], own2[n]]

            self.spread(4, 1, piece, piece)
        elif k == 5:
            self.wait(4)

            def piece(n, part, _):
                return self.fin.at[h, part, own[n]]

            self.spread(5, 0, piece, piece)
        elif k == 6:
            self.wait(5)
            self.copy(6, 0, self.fin.at[h], self.fin.at[h], self.p.twin())
        elif k == 7:
            self.wait(6)

    def drain(self):
        for group in self.copies.values():
            for c in group:
                c.wait_send()


class Vectors:
    def __init__(self, place, val, slots, send, recv):
        self.p, self.val, self.slots, self.send, self.recv = place, val, slots, send, recv
        self.copies = []

    def start(self, k):
        axis = k - 1
        hops = ((0, self.p.twin()),) if k == 0 else tuple(
            (d, self.p.shifted(jnp.int32(axis), d)) for d in (1, 2, 3)
        )
        for d, device in hops:
            at = 0 if k == 0 else 3 * (k - 1) + d
            c = pltpu.make_async_remote_copy(
                src_ref=self.val.at[k],
                dst_ref=self.slots.at[at],
                send_sem=self.send.at[at],
                recv_sem=self.recv.at[at],
                device_id=device,
                device_id_type=MESH,
            )
            c.start()
            self.copies.append((k, c))

    def finish(self, k):
        for j, c in self.copies:
            if j == k:
                c.wait_recv()
        if k == 0:
            self.val[1] = self.val[0] + self.slots[0]
        else:
            at = 3 * (k - 1)
            near = self.val[k] + self.slots[at + 2]
            far = self.slots[at + 1] + self.slots[at + 3]
            self.val[k + 1] = near + far

    def drain(self):
        for _, c in self.copies:
            c.wait_send()


def layer(
    nodes_h, edges_h, senders, receivers, live, send_rows, cot_h,
    wei_h, eib, weo_h, eob, egain, wni_h, nib, wno_h, nob, ngain,
    new_nodes_h, node_grad_h, edge_grad_h, fin_a_h, fin_o_h, fin_b_h, fin_c_h, vec_h,
    nodes, edges, cot, wei, weo, wni, wno,
    ohs, oht, ohr, edges_t, pre, hid, normed, scale, prnd, staging, post,
    table, grad_rows, zb, halo_out, halo_in, back_out, back_in, sendt,
    new_nodes, node_base, node_grad, summed, sum_acc, outer_acc,
    npre, npost, nhid, npost_round, npre_round, acc,
    bufs_a, bufs_o, bufs_b, bufs_c, vec, vec_slots,
    in_sem, out_sem, halo_send, halo_recv, sems_a, sems_o, sems_b, sems_c, sems_v,
):
    place = Place()
    prd = ohs

    def load(k, src, dst):
        c = pltpu.make_async_copy(src, dst, in_sem.at[k])
        c.start()
        return c

    def store(k, src, dst):
        c = pltpu.make_async_copy(src, dst, out_sem.at[k])
        c.start()
        return c

    c_nodes = load(0, nodes_h, nodes)
    c_wei = load(1, wei_h, wei)
    c_edges = load(2, edges_h, edges)
    c_wni = load(4, wni_h, wni)
    c_weo = load(3, weo_h, weo)
    c_wno = load(5, wno_h, wno)
    c_cot = load(6, cot_h, cot)

    barrier = pltpu.get_barrier_semaphore()
    partners = [place.neighbour(n) for n in range(8)] + [place.twin()]
    for axis in range(3):
        for d in (1, 2, 3):
            partners.append(place.shifted(jnp.int32(axis), d))
    for device in partners:
        pl.semaphore_signal(barrier, inc=1, device_id=device, device_id_type=MESH)

    thirds = (slice(0, 1), slice(1, 2), slice(2, 3))
    red_a = Reduce(place, thirds, *bufs_a, *sems_a)
    red_o = Reduce(place, (slice(0, 2), slice(2, 3), slice(3, 4)), *bufs_o, *sems_o)
    red_b = Reduce(place, thirds, *bufs_b, *sems_b)
    red_c = Reduce(place, thirds, *bufs_c, *sems_c)
    red_v = Vectors(place, vec, vec_slots, *sems_v)

    picks = []
    for k in range(2):
        col = column_of(send_rows[:, k * LANE : (k + 1) * LANE])
        picks.append(jnp.concatenate([hot(col == lanes(j * LANE)) for j in range(4)], axis=1))
    picks = jnp.concatenate(picks, axis=0)
    c_nodes.wait()
    halo_out[...] = dot(picks, nodes[...]).astype(BF16).reshape(8, SLOT, D)
    pl.semaphore_wait(barrier, len(partners))

    def exchange(src, dst, base):
        copies = []
        for n in range(8):
            c = pltpu.make_async_remote_copy(
                src_ref=src.at[n],
                dst_ref=dst.at[7 - n],
                send_sem=halo_send.at[base + n],
                recv_sem=halo_recv.at[base + 7 - n],
                device_id=place.neighbour(n),
                device_id_type=MESH,
            )
            c.start()
            copies.append(c)
        return copies

    halo = exchange(halo_out, halo_in, 0)

    rowi = lax.broadcasted_iota(I32, (NODE, LANE), 0)
    for k in range(2):
        row = send_rows[:, k * LANE : (k + 1) * LANE]
        sendt[:, k * LANE : (k + 1) * LANE] = hot(rowi == row)
    acc[...] = jnp.zeros_like(acc)
    c_wei.wait()
    table[0:NODE, :] = dot(nodes[...], wei[D : 2 * D, :]).astype(BF16)
    table[TABLE:WIDE, :] = dot(nodes[...], wei[2 * D : 3 * D, :]).astype(BF16)
    c_edges.wait()

    def early(c, _):
        base = pl.multiple_of(c * CHUNK, CHUNK)
        rows = pl.ds(base, CHUNK)
        pre[rows, :] = dot(edges[rows, :], wei[0:D, :]) + eib[...]
        edges_t[:, rows] = jnp.transpose(edges[rows, :])
        for j in range(CHUNK // LANE):
            s_row = senders[pl.ds(c * (CHUNK // LANE) + j, 1), :]
            r_row = receivers[pl.ds(c * (CHUNK // LANE) + j, 1), :]
            s_col, r_col = column_of(s_row), column_of(r_row)
            here = pl.ds(pl.multiple_of(base + j * LANE, LANE), LANE)
            for k in range(TABLE // LANE):
                ohs[here, k * LANE : (k + 1) * LANE] = hot(s_col == lanes(k * LANE))
            for k in range(NODE // LANE):
                ohr[here, k * LANE : (k + 1) * LANE] = hot(r_col == lanes(k * LANE))
            ids = lax.broadcasted_iota(I32, (TABLE, LANE), 0)
            oht[0:TABLE, here] = hot(ids == s_row)
            oht[TABLE:WIDE, here] = hot(rowi == r_row)
        return 0

    lax.fori_loop(0, STEPS, early, 0)
    c_wni.wait()
    npre[...] = dot(nodes[...], wni[0:D, :]) + nib[...]
    c_weo.wait()
    c_wno.wait()
    c_cot.wait()

    for c in halo:
        c.wait_recv()
    table[NODE:TABLE, :] = dot(halo_in[...].reshape(PEER, D), wei[D : 2 * D, :]).astype(BF16)

    def part(t, s):
        return slice(t * PART + s * SUB, t * PART + (s + 1) * SUB)

    def whole(t):
        return slice(t * PART, (t + 1) * PART)

    def live_rows(t, s):
        ids = lax.broadcasted_iota(I32, (SUB, LANE), 0)
        one = jnp.where(ids < live[0] - (t * PART + s * SUB), 1.0, 0.0)
        return jnp.concatenate([one] * (D // LANE), axis=1)

    def fwd_gather(t):
        rows = whole(t)
        z = dot(ohs[rows, :], table[0:TABLE, :]) + dot(ohr[rows, :], table[TABLE:WIDE, :])
        pre[rows, :] += z

    def fwd_silu(t):
        for s in range(SUBS):
            rows = part(t, s)
            h, slope = silu_parts(pre[rows, :])
            hid[rows, :] = h.astype(BF16)
            pre[rows, :] = slope

    def fwd_outer(t):
        post[t % 3] = dot(hid[whole(t), :], weo[...])

    def fwd_norm(t):
        for s in range(SUBS):
            rows = part(t, s)
            unit, inv = normalize(post[t % 3, s * SUB : (s + 1) * SUB, :] + eob[...])
            normed[rows, :] = unit.astype(BF16)
            scale[rows, :] = inv
            new = edges[rows, :].astype(F32) + unit * egain[...]
            prnd[rows, :] = (new * live_rows(t, s)).astype(BF16)

    def fwd_sum(t):
        got = dot(oht[TABLE:WIDE, whole(t)], prnd[whole(t), :])
        if t == 0:
            sum_acc[...] = got
        else:
            sum_acc[...] += got

    def at(f, t):
        if 0 <= t < PARTS:
            f(t)

    for t in range(PARTS + 3):
        at(fwd_gather, t)
        at(fwd_silu, t - 1)
        at(fwd_norm, t - 2)
        at(fwd_outer, t - 1)
        at(fwd_sum, t - 3)
    summed[...] = sum_acc[...].astype(BF16)

    def fold(x):
        return jnp.sum(x.reshape(x.shape[0] // 8, 8, x.shape[1]), axis=0)

    halves = (0, 1)
    for t in halves:
        npre[whole(t), :] += dot(summed[whole(t), :], wni[D : 2 * D, :])
    for t in halves:
        for s in range(SUBS):
            rows = part(t, s)
            h, slope = silu_parts(npre[rows, :])
            nhid[rows, :] = h.astype(BF16)
            npre[rows, :] = slope
        npost[whole(t), :] = dot(nhid[whole(t), :], wno[...])
    for t in halves:
        for s in range(SUBS):
            rows = part(t, s)
            unit, inv = normalize(npost[rows, :] + nob[...])
            new_nodes[rows, :] = (nodes[rows, :].astype(F32) + unit * ngain[...]).astype(BF16)
            cotangent = cot[rows, :].astype(F32)
            acc[5] += fold(cotangent * unit)
            grad = norm_back(cotangent * ngain[...], unit, inv)
            acc[4] += fold(grad)
            npost_round[rows, :] = grad.astype(BF16)
        grad = dot_rt(npost_round[whole(t), :], wno[...]) * npre[whole(t), :]
        acc[3] += fold(grad)
        npre_round[whole(t), :] = grad.astype(BF16)
    for t in halves:
        grad_rows[whole(t), :] = dot_rt(npre_round[whole(t), :], wni[D : 2 * D, :]).astype(BF16)
    s_nodes = store(0, new_nodes, new_nodes_h)

    def bwd_gather(t):
        post[t % 3] = dot(ohr[whole(t), :], grad_rows[...])

    def bwd_norm(t):
        for s in range(SUBS):
            rows = part(t, s)
            g = post[t % 3, s * SUB : (s + 1) * SUB, :] * live_rows(t, s)
            unit = normed[rows, :].astype(F32)
            acc[2] += fold(g * unit)
            grad = norm_back(g * egain[...], unit, scale[rows, :])
            acc[1] += fold(grad)
            prnd[rows, :] = grad.astype(BF16)

    def bwd_outer(t):
        rows = slice((t - 1) * PART, (t + 1) * PART)
        got = dot_lt(hid[rows, :], prnd[rows, :])
        if t == 1:
            outer_acc[...] = got
        else:
            outer_acc[...] += got

    for t in range(PARTS + 1):
        at(bwd_gather, t)
        at(bwd_norm, t - 1)
        if t == 1:
            red_a.pack(2, dot_lt(nhid[...], npost_round[...]))
        if t == 2:
            red_a.pack(0, dot_lt(nodes[...], npre_round[...]))
        if t == 3:
            red_a.pack(1, dot_lt(summed[...], npre_round[...]))
            red_a.step(0)
        if t == 4:
            node_base[...] = cot[...].astype(F32) + dot_rt(npre_round[...], wni[0:D, :])
        if t >= 4 and t % 2 == 0:
            bwd_outer(t - 3)
    red_a.step(1)
    bwd_outer(PARTS - 1)
    for j in range(4):
        red_o.pack(j, outer_acc[:, j * LANE : (j + 1) * LANE])
    red_o.step(0)

    def bwd_inner(t, cols):
        grad = dot_rt(prnd[whole(t), :], weo[cols, :]) * pre[whole(t), cols]
        acc[0, :, cols] += fold(grad)
        prd[whole(t), cols] = grad.astype(BF16)

    left, right = slice(0, D // 2), slice(D // 2, D)
    for t in range(PARTS):
        bwd_inner(t, left)

    def z_rows(j, cols):
        zb[j * PART : (j + 1) * PART, cols] = dot(
            oht[j * PART : (j + 1) * PART, :], prd[:, cols]
        ).astype(BF16)

    def inner_sums(red, cols):
        incoming = halo_in[...].reshape(PEER, D)
        red.pack(1, dot_lt(nodes[...], zb[0:NODE, cols]) + dot_lt(incoming, zb[NODE:TABLE, cols]))
        red.pack(2, dot_lt(nodes[...], zb[TABLE:WIDE, cols]))
        red.step(0)

    for j in range(WIDE // PART):
        z_rows(j, left)
        bwd_inner(j, right)
    for t in range(WIDE // PART, PARTS):
        bwd_inner(t, right)
    red_b.pack(0, dot(edges_t[...], prd[:, left]))
    inner_sums(red_b, left)
    red_a.step(2)
    red_o.step(1)
    vec[0, 0:6, :] = jnp.sum(acc[...], axis=1)
    vec[0, 6:8, :] = jnp.zeros((2, D), F32)
    red_v.start(0)
    for j in range(WIDE // PART):
        z_rows(j, right)
    red_b.step(1)
    red_c.pack(0, dot(edges_t[...], prd[:, right]))
    inner_sums(red_c, right)
    red_a.step(3)
    red_o.step(2)
    red_v.finish(0)
    red_v.start(1)

    back = dot_rt(zb[NODE:TABLE, :], wei[D : 2 * D, :]).astype(BF16)
    back_out[...] = back.reshape(8, SLOT, D)
    returning = exchange(back_out, back_in, 8)
    red_a.step(4)
    red_c.step(1)
    red_o.step(3)
    red_b.step(2)
    stores = []

    def edge_out(c):
        rows = pl.ds(c * CHUNK, CHUNK)
        grad = dot_rt(prd[rows, 0:D], wei[0:D, :]) + dot(ohr[rows, :], grad_rows[...])
        alive = lax.broadcasted_iota(I32, (CHUNK, D), 0) < live[0] - c * CHUNK
        staging[rows, :] = jnp.where(alive, grad, 0.0).astype(BF16)
        stores.append(store(2 + c, staging.at[rows], edge_grad_h.at[rows]))

    edge_out(0)
    red_v.finish(1)
    red_v.start(2)
    red_a.step(5)
    red_b.step(3)
    red_o.step(4)
    red_c.step(2)
    edge_out(1)
    red_b.step(4)
    red_o.step(5)
    red_c.step(3)
    edge_out(2)
    red_v.finish(2)
    red_v.start(3)
    red_b.step(5)
    red_c.step(4)
    red_o.step(6)
    edge_out(3)
    red_a.step(6)
    red_c.step(5)
    node_base[...] += dot_rt(zb[0:NODE, :], wei[D : 2 * D, :])
    node_base[...] += dot_rt(zb[TABLE:WIDE, :], wei[2 * D : 3 * D, :])
    for c in returning:
        c.wait_recv()
    owned = dot(sendt[...], back_in[...].reshape(PEER, D))
    node_grad[...] = (node_base[...] + owned).astype(BF16)
    stores.append(store(1, node_grad, node_grad_h))
    red_v.finish(3)
    stores.append(store(6, vec.at[4], vec_h))
    red_b.step(6)
    red_o.step(7)
    stores.append(store(8, red_o.fin, fin_o_h))
    red_a.step(7)
    stores.append(store(7, red_a.fin, fin_a_h))
    red_c.step(6)
    red_b.step(7)
    stores.append(store(9, red_b.fin, fin_b_h))
    red_c.step(7)
    stores.append(store(10, red_c.fin, fin_c_h))
    for c in halo + returning:
        c.wait_send()
    for red in (red_a, red_o, red_b, red_c, red_v):
        red.drain()
    s_nodes.wait()
    for c in stores:
        c.wait()


def fin_shape(nb, width):
    return (2, nb, 4, 4, 16, width)


FINS = ((3, D), (4, LANE), (3, D // 2), (3, D // 2))


def reduce_bufs(nb, width):
    tile = (16, width)
    return (
        pltpu.VMEM(fin_shape(nb, width), BF16),
        pltpu.VMEM((nb, 4, 4) + tile, BF16),
        pltpu.VMEM((nb, 4, 4) + tile, BF16),
        pltpu.VMEM((3, nb, 4) + tile, BF16),
        pltpu.VMEM((nb, 4) + tile, BF16),
        pltpu.VMEM((3, nb) + tile, BF16),
        pltpu.VMEM((nb,) + tile, BF16),
        pltpu.VMEM((3, nb) + tile, BF16),
        pltpu.VMEM(fin_shape(nb, width), BF16),
    )


def sem_pair(n):
    return (pltpu.SemaphoreType.DMA((n,)), pltpu.SemaphoreType.DMA((n,)))


def widen(
    fa, fo, fb, fc, vec, new_nodes, node_grad, edge_grad,
    new_nodes_o, node_grad_o, edge_grad_o, edge_inner, edge_outer, node_inner, node_outer,
    v0, v1, v2, v3, v4, v5,
    va, vo, vb, vc, vn, vg, ve, wide, in_sem, out_sem,
):
    outs = []

    def load(k, src, dst):
        c = pltpu.make_async_copy(src, dst, in_sem.at[k])
        c.start()
        return c

    def store(k, src, dst):
        c = pltpu.make_async_copy(src, dst, out_sem.at[k])
        c.start()
        outs.append(c)

    c_a = [load(h, fa.at[h], va.at[h]) for h in range(2)]
    c_b = [load(2 + h, fb.at[h], vb.at[h]) for h in range(2)]
    c_c = [load(4 + h, fc.at[h], vc.at[h]) for h in range(2)]
    c_o = load(6, fo, vo)
    c_e = [load(7 + k, edge_grad.at[pl.ds(k * 512, 512)], ve.at[pl.ds(k * 512, 512)]) for k in range(4)]
    c_n = load(11, new_nodes, vn)
    c_g = load(12, node_grad, vg)
    k_out = 0
    HALF = NODE // 2

    places = ((node_inner, 0), (node_inner, 512), (node_outer, 0))
    for h in range(2):
        c_a[h].wait()
        for j, (out, first) in enumerate(places):
            rows = pl.ds(j * 512 + h * HALF, HALF)
            wide[rows, :] = va[h, j].reshape(HALF, D).astype(F32)
            store(k_out, wide.at[rows], out.at[pl.ds(first + h * HALF, HALF)])
            k_out += 1
    for h in range(2):
        c_b[h].wait()
        c_c[h].wait()
        for j in range(3):
            rows = pl.ds(1536 + j * 512 + h * HALF, HALF)
            wide[rows, 0:HALF] = vb[h, j].reshape(HALF, HALF).astype(F32)
            wide[rows, HALF:D] = vc[h, j].reshape(HALF, HALF).astype(F32)
            store(k_out, wide.at[rows], edge_inner.at[pl.ds(j * 512 + h * HALF, HALF)])
            k_out += 1
    c_o.wait()
    for h in range(2):
        rows = pl.ds(3072 + h * HALF, HALF)
        for j in range(4):
            wide[rows, j * LANE : (j + 1) * LANE] = vo[h, j].reshape(HALF, LANE).astype(F32)
        store(k_out, wide.at[rows], edge_outer.at[pl.ds(h * HALF, HALF)])
        k_out += 1
    for k in range(4):
        c_e[k].wait()
        store(k_out, ve.at[pl.ds(k * 512, 512)], edge_grad_o.at[pl.ds(k * 512, 512)])
        k_out += 1
    c_n.wait()
    store(k_out, vn, new_nodes_o)
    c_g.wait()
    store(k_out + 1, vg, node_grad_o)
    for k, out in enumerate((v0, v1, v2, v3, v4, v5)):
        out[...] = vec[k : k + 1, :]
    for c in outs:
        c.wait()


def unpack(outs):
    new_nodes, node_grad, edge_grad, fa, fo, fb, fc, vec = outs
    hbm = pl.BlockSpec(memory_space=pl.ANY)
    vm = pl.BlockSpec(memory_space=pltpu.VMEM)
    shapes = [
        ((NODE, D), BF16), ((NODE, D), BF16), ((EDGE, D), BF16),
        ((3 * D, D), F32), ((D, D), F32), ((2 * D, D), F32), ((D, D), F32),
    ] + [((1, D), F32)] * 6
    scratch = [pltpu.VMEM(fin_shape(*f), BF16) for f in FINS]
    return pl.pallas_call(
        widen,
        out_shape=[jax.ShapeDtypeStruct(s, t) for s, t in shapes],
        in_specs=[hbm] * 4 + [vm] + [hbm] * 3,
        out_specs=[hbm] * 7 + [vm] * 6,
        scratch_shapes=scratch + [
            pltpu.VMEM((NODE, D), BF16), pltpu.VMEM((NODE, D), BF16), pltpu.VMEM((EDGE, D), BF16),
            pltpu.VMEM((7 * D, D), F32),
            pltpu.SemaphoreType.DMA((13,)), pltpu.SemaphoreType.DMA((20,)),
        ],
        compiler_params=pltpu.CompilerParams(vmem_limit_bytes=63 * 2**20),
        name="widen",
    )(fa, fo, fb, fc, vec, new_nodes, node_grad, edge_grad)


def body(
    node_states, edge_states, senders, receivers, live_count, send_rows, node_cotangent,
    edge_inner, edge_inbias, edge_outer, edge_outbias, edge_gain,
    node_inner, node_inbias, node_outer, node_outbias, node_gain,
):
    hbm = pl.BlockSpec(memory_space=pl.ANY)
    vm = pl.BlockSpec(memory_space=pltpu.VMEM)
    sm = pl.BlockSpec(memory_space=pltpu.SMEM)

    def row(v):
        return v.reshape(1, D)

    def v(shape, dtype=BF16):
        return pltpu.VMEM(shape, dtype)

    outs = pl.pallas_call(
        layer,
        out_shape=[
            jax.ShapeDtypeStruct((NODE, D), BF16),
            jax.ShapeDtypeStruct((NODE, D), BF16),
            jax.ShapeDtypeStruct((EDGE, D), BF16),
        ]
        + [jax.ShapeDtypeStruct(fin_shape(*f), BF16) for f in FINS]
        + [jax.ShapeDtypeStruct((8, D), F32)],
        in_specs=[
            hbm, hbm, vm, vm, sm, vm, hbm,
            hbm, vm, hbm, vm, vm, hbm, vm, hbm, vm, vm,
        ],
        out_specs=[hbm] * 8,
        scratch_shapes=[
            v((NODE, D)), v((EDGE, D)), v((NODE, D)),
            v((3 * D, D)), v((D, D)), v((2 * D, D)), v((D, D)),
            v((EDGE, TABLE)), v((WIDE, EDGE)), v((EDGE, NODE)), v((D, EDGE)),
            v((EDGE, D), F32), v((EDGE, D)), v((EDGE, D)), v((EDGE, 1), F32),
            v((EDGE, D)), v((EDGE, D)), v((3, PART, D), F32),
            v((WIDE, D)), v((NODE, D)), v((WIDE, D)),
            v((8, SLOT, D)), v((8, SLOT, D)), v((8, SLOT, D)), v((8, SLOT, D)),
            v((NODE, PEER)),
            v((NODE, D)), v((NODE, D), F32), v((NODE, D)), v((NODE, D)),
            v((NODE, D), F32), v((D, D), F32),
            v((NODE, D), F32), v((NODE, D), F32), v((NODE, D)), v((NODE, D)), v((NODE, D)),
            v((6, 8, D), F32),
        ]
        + [reduce_bufs(*f) for f in FINS]
        + [
            v((5, 8, D), F32), v((10, 8, D), F32),
            pltpu.SemaphoreType.DMA((7,)), pltpu.SemaphoreType.DMA((11,)),
            pltpu.SemaphoreType.DMA((16,)), pltpu.SemaphoreType.DMA((16,)),
            sem_pair(47), sem_pair(47), sem_pair(47), sem_pair(47), sem_pair(10),
        ],
        compiler_params=pltpu.CompilerParams(
            collective_id=0, has_side_effects=True, vmem_limit_bytes=63 * 2**20
        ),
        name="layer",
    )(
        node_states, edge_states, senders.reshape(16, LANE), receivers.reshape(16, LANE),
        live_count, send_rows, node_cotangent,
        edge_inner, row(edge_inbias), edge_outer, row(edge_outbias), row(edge_gain),
        node_inner, row(node_inbias), node_outer, row(node_outbias), row(node_gain),
    )
    new_nodes, node_grad, edge_grad, ei, eo, ni, no, *vecs = unpack(outs)
    vecs = [x.reshape(D) for x in vecs]
    return (
        new_nodes, node_grad, edge_grad,
        ei, vecs[0], eo, vecs[1], vecs[2],
        ni, vecs[3], no, vecs[4], vecs[5],
    )


def solution(mesh):
    nodes = P(("lat", "lon"), None)
    flat = P(("lat", "lon"))
    return jax.shard_map(
        body,
        mesh=mesh,
        in_specs=(nodes, nodes, flat, flat, flat, nodes, nodes) + (P(),) * 10,
        out_specs=(nodes, nodes, nodes) + (P(),) * 10,
        check_vma=False,
    )
```

```python
import functools

import jax
import jax.numpy as jnp
from jax import lax
from jax.experimental import pallas as pl
from jax.experimental.pallas import tpu as pltpu
from jax.sharding import PartitionSpec as P

MESH = pl.DeviceIdType.MESH
F32 = jnp.float32
BF16 = jnp.bfloat16
I32 = jnp.int32
epsilon = 1e-05

D = 512
NODE = 512
EDGE = 2048
SLOT = 32
PEER = 256
TABLE = NODE + PEER
WIDE = TABLE + NODE
CHUNK = 512
STEPS = EDGE // CHUNK
PART = 512
NPART = 256
NSUBS = NPART // 32
TALL = NODE + PEER + NODE + D
PARTS = EDGE // PART
SUB = 32
SUBS = PART // SUB
LANE = 128
N_LAT = 8
N_LON = 16
OFFSETS = ((-1, -1), (-1, 0), (-1, 1), (0, -1), (0, 1), (1, -1), (1, 0), (1, 1))


def dot(a, b):
    return jnp.dot(a, b, preferred_element_type=F32)


def dot_rt(a, b):
    return lax.dot_general(a, b, (((1,), (1,)), ((), ())), preferred_element_type=F32)


def dot_lt(a, b):
    return lax.dot_general(a, b, (((0,), (0,)), ((), ())), preferred_element_type=F32)


def row_mean(x):
    return jnp.sum(x, axis=-1, keepdims=True) * (1.0 / D)


def col_sum(x):
    return jnp.sum(x, axis=0, keepdims=True)


def silu_parts(z):
    sig = 0.5 + 0.5 * jnp.tanh(0.5 * z)
    h = z * sig
    return h, sig + h * (1.0 - sig)


def normalize(post):
    centered = post - row_mean(post)
    scale = lax.rsqrt(row_mean(centered * centered) + epsilon)
    return centered * scale, scale


def norm_back(t, normed, scale):
    return scale * (t - row_mean(t) - normed * row_mean(t * normed))


def column_of(row):
    return jnp.transpose(jnp.broadcast_to(row.astype(F32), (LANE, LANE))).astype(I32)


def lanes(base):
    return lax.broadcasted_iota(I32, (LANE, LANE), 1) + base


def hot(mask):
    return jnp.where(mask, 1.0, 0.0).astype(BF16)


class Place:
    def __init__(self):
        self.lat = lax.axis_index("lat")
        self.lon = lax.axis_index("lon")
        self.core = lax.rem(self.lat, 2)
        self.y = lax.div(self.lat, 2)
        self.x = lax.div(self.lon, 4)
        self.z = lax.rem(self.lon, 4)

    def neighbour(self, n):
        dlat, dlon = OFFSETS[n]
        return (
            lax.rem(self.lat + (dlat + N_LAT), N_LAT),
            lax.rem(self.lon + (dlon + N_LON), N_LON),
        )

    def twin(self):
        return (self.y * 2 + (1 - self.core), self.lon)

    def index(self, axis):
        is_x = lax.div((2 - axis) * (1 - axis), 2)
        is_y = axis * (2 - axis)
        is_z = lax.div(axis * (axis - 1), 2)
        return self.x * is_x + self.y * is_y + self.z * is_z

    def shifted(self, axis, d):
        is_x = lax.div((2 - axis) * (1 - axis), 2)
        is_y = axis * (2 - axis)
        is_z = lax.div(axis * (axis - 1), 2)
        x = lax.rem(self.x + d * is_x, 4)
        y = lax.rem(self.y + d * is_y, 4)
        z = lax.rem(self.z + d * is_z, 4)
        return (y * 2 + self.core, x * 4 + z)

    def axis(self, b, level):
        return lax.rem(self.core + (b + level), 3)


class Reduce:
    def __init__(self, place, streams, gb, rc, s0, r1, s1, r2, s2, r3, fin, send, recv):
        self.p, self.streams = place, streams
        self.gb, self.rc, self.s0, self.r1, self.s1 = gb, rc, s0, r1, s1
        self.r2, self.s2, self.r3, self.fin = r2, s2, r3, fin
        self.send, self.recv = send, recv
        self.copies = {}

    def pack(self, j, val):
        width = val.shape[1]
        self.gb[:, j] = val.astype(BF16).reshape(2, 4, 4, 16, width)

    def copy(self, step, k, src, dst, device):
        at = 1 + (step - 1) * 9 + k if 1 <= step <= 5 else (0 if step == 0 else 46)
        c = pltpu.make_async_remote_copy(
            src_ref=src,
            dst_ref=dst,
            send_sem=self.send.at[at],
            recv_sem=self.recv.at[at],
            device_id=device,
            device_id_type=MESH,
        )
        c.start()
        self.copies.setdefault(step, []).append(c)

    def wait(self, step):
        for c in self.copies[step]:
            c.wait_recv()

    def spread(self, step, level, src, dst):
        for n, part in enumerate(self.streams):
            axis = self.p.axis(n, level)
            for d in (2, 1, 3):
                there = lax.rem(self.p.index(axis) + d, 4)
                self.copy(
                    step, n * 3 + d - 1, src(n, part, there), dst(n, part, d), self.p.shifted(axis, d)
                )

    def step(self, k):
        h = self.p.core
        count = len(self.streams)
        own = [self.p.index(self.p.axis(n, 0)) for n in range(count)]
        own2 = [self.p.index(self.p.axis(n, 1)) for n in range(count)]
        if k == 0:
            self.copy(0, 0, self.gb.at[1 - h], self.rc, self.p.twin())
        elif k == 1:
            self.wait(0)
            for part in self.streams:
                mine = self.gb[h, part].astype(F32)
                self.s0[part] = (mine + self.rc[part].astype(F32)).astype(BF16)
            self.spread(
                1, 0, lambda n, part, i: self.s0.at[part, i], lambda n, part, d: self.r1.at[d - 1, part]
            )
        elif k == 2:
            self.wait(1)
            for n, part in enumerate(self.streams):
                total = self.s0[part, own[n]].astype(F32)
                for d in range(3):
                    total += self.r1[d, part].astype(F32)
                self.s1[part] = total.astype(BF16)
            self.spread(
                2, 1, lambda n, part, i: self.s1.at[part, i], lambda n, part, d: self.r2.at[d - 1, part]
            )
        elif k == 3:
            self.wait(2)
            for n, part in enumerate(self.streams):
                total = self.s1[part, own2[n]].astype(F32)
                for d in range(3):
                    total += self.r2[d, part].astype(F32)
                self.s2[part] = total.astype(BF16)
            self.spread(
                3, 2, lambda n, part, i: self.s2.at[part], lambda n, part, d: self.r3.at[d - 1, part]
            )
        elif k == 4:
            self.wait(3)
            for n, part in enumerate(self.streams):
                near = self.s2[part].astype(F32) + self.r3[1, part].astype(F32)
                far = self.r3[0, part].astype(F32) + self.r3[2, part].astype(F32)
                self.fin[h, part, own[n], own2[n]] = (near + far).astype(BF16)

            def piece(n, part, _):
                return self.fin.at[h, part, own[n], own2[n]]

            self.spread(4, 1, piece, piece)
        elif k == 5:
            self.wait(4)

            def piece(n, part, _):
                return self.fin.at[h, part, own[n]]

            self.spread(5, 0, piece, piece)
        elif k == 6:
            self.wait(5)
            self.copy(6, 0, self.fin.at[h], self.fin.at[h], self.p.twin())
        elif k == 7:
            self.wait(6)

    def drain(self):
        for group in self.copies.values():
            for c in group:
                c.wait_send()


class Vectors:
    def __init__(self, place, val, slots, send, recv):
        self.p, self.val, self.slots, self.send, self.recv = place, val, slots, send, recv
        self.copies = []

    def start(self, k):
        axis = k - 1
        hops = ((0, self.p.twin()),) if k == 0 else tuple(
            (d, self.p.shifted(jnp.int32(axis), d)) for d in (1, 2, 3)
        )
        for d, device in hops:
            at = 0 if k == 0 else 3 * (k - 1) + d
            c = pltpu.make_async_remote_copy(
                src_ref=self.val.at[k],
                dst_ref=self.slots.at[at],
                send_sem=self.send.at[at],
                recv_sem=self.recv.at[at],
                device_id=device,
                device_id_type=MESH,
            )
            c.start()
            self.copies.append((k, c))

    def finish(self, k):
        for j, c in self.copies:
            if j == k:
                c.wait_recv()
        if k == 0:
            self.val[1] = self.val[0] + self.slots[0]
        else:
            at = 3 * (k - 1)
            near = self.val[k] + self.slots[at + 2]
            far = self.slots[at + 1] + self.slots[at + 3]
            self.val[k + 1] = near + far

    def drain(self):
        for _, c in self.copies:
            c.wait_send()


def layer(
    nodes_h, edges_h, senders, receivers, live, send_rows, cot_h,
    wei_h, eib, weo_h, eob, egain, wni_h, nib, wno_h, nob, ngain,
    new_nodes_h, node_grad_h, edge_grad_h, fin_a_h, fin_b_h, fin_c_h, vec_h,
    nodes, edges, cot, wei, weo, wni, wno,
    ohs, oht, ohr, pre, hid, normed, scale, prnd, staging, post,
    table, grad_rows, zb, halo_out, halo_in, back_out, back_in, sendt,
    new_nodes, node_base, node_grad, summed, sum_acc, outer_acc,
    npre, npost, nhid, npost_round, npre_round, acc,
    bufs_a, bufs_b, bufs_c, vec, vec_slots,
    in_sem, out_sem, halo_send, halo_recv, sems_a, sems_b, sems_c, sems_v,
):
    place = Place()
    prd = ohs

    def load(k, src, dst):
        c = pltpu.make_async_copy(src, dst, in_sem.at[k])
        c.start()
        return c

    def store(k, src, dst):
        c = pltpu.make_async_copy(src, dst, out_sem.at[k])
        c.start()
        return c

    c_nodes = load(0, nodes_h, nodes)
    c_wei = load(1, wei_h, wei)
    c_edges = load(2, edges_h, edges)
    c_wni = load(4, wni_h, wni)
    c_weo = load(3, weo_h, weo)
    c_wno = load(5, wno_h, wno)
    c_cot = load(6, cot_h, cot)

    barrier = pltpu.get_barrier_semaphore()
    partners = [place.neighbour(n) for n in range(8)] + [place.twin()]
    for axis in range(3):
        for d in (1, 2, 3):
            partners.append(place.shifted(jnp.int32(axis), d))
    for device in partners:
        pl.semaphore_signal(barrier, inc=1, device_id=device, device_id_type=MESH)

    thirds = (slice(0, 1), slice(1, 2), slice(2, 3))
    red_a = Reduce(place, thirds, *bufs_a, *sems_a)
    red_b = Reduce(place, (slice(0, 2), slice(2, 4), slice(4, 5)), *bufs_b, *sems_b)
    red_c = Reduce(place, thirds, *bufs_c, *sems_c)
    red_v = Vectors(place, vec, vec_slots, *sems_v)

    picks = []
    for k in range(2):
        col = column_of(send_rows[:, k * LANE : (k + 1) * LANE])
        picks.append(jnp.concatenate([hot(col == lanes(j * LANE)) for j in range(4)], axis=1))
    picks = jnp.concatenate(picks, axis=0)
    c_nodes.wait()
    halo_out[...] = dot(picks, nodes[...]).astype(BF16).reshape(8, SLOT, D)
    pl.semaphore_wait(barrier, len(partners))

    def exchange(src, dst, base):
        copies = []
        for n in range(8):
            c = pltpu.make_async_remote_copy(
                src_ref=src.at[n],
                dst_ref=dst.at[7 - n],
                send_sem=halo_send.at[base + n],
                recv_sem=halo_recv.at[base + 7 - n],
                device_id=place.neighbour(n),
                device_id_type=MESH,
            )
            c.start()
            copies.append(c)
        return copies

    halo = exchange(halo_out, halo_in, 0)

    rowi = lax.broadcasted_iota(I32, (NODE, LANE), 0)
    for k in range(2):
        row = send_rows[:, k * LANE : (k + 1) * LANE]
        sendt[:, k * LANE : (k + 1) * LANE] = hot(rowi == row)
    acc[...] = jnp.zeros_like(acc)
    c_wei.wait()
    table[0:NODE, :] = dot(nodes[...], wei[D : 2 * D, :]).astype(BF16)
    table[TABLE:WIDE, :] = dot(nodes[...], wei[2 * D : 3 * D, :]).astype(BF16)
    c_edges.wait()

    def early(c, _):
        base = pl.multiple_of(c * CHUNK, CHUNK)
        rows = pl.ds(base, CHUNK)
        pre[rows, :] = dot(edges[rows, :], wei[0:D, :]) + eib[...]
        oht[WIDE:TALL, rows] = jnp.transpose(edges[rows, :])
        for j in range(CHUNK // LANE):
            s_row = senders[pl.ds(c * (CHUNK // LANE) + j, 1), :]
            r_row = receivers[pl.ds(c * (CHUNK // LANE) + j, 1), :]
            s_col, r_col = column_of(s_row), column_of(r_row)
            here = pl.ds(pl.multiple_of(base + j * LANE, LANE), LANE)
            for k in range(TABLE // LANE):
                ohs[here, k * LANE : (k + 1) * LANE] = hot(s_col == lanes(k * LANE))
            for k in range(NODE // LANE):
                ohr[here, k * LANE : (k + 1) * LANE] = hot(r_col == lanes(k * LANE))
            ids = lax.broadcasted_iota(I32, (TABLE, LANE), 0)
            oht[0:TABLE, here] = hot(ids == s_row)
            oht[TABLE:WIDE, here] = hot(rowi == r_row)
        return 0

    lax.fori_loop(0, STEPS, early, 0)
    c_wni.wait()
    npre[...] = dot(nodes[...], wni[0:D, :]) + nib[...]
    c_weo.wait()
    c_wno.wait()
    c_cot.wait()

    for c in halo:
        c.wait_recv()
    table[NODE:TABLE, :] = dot(halo_in[...].reshape(PEER, D), wei[D : 2 * D, :]).astype(BF16)

    def part(t, s):
        return slice(t * PART + s * SUB, t * PART + (s + 1) * SUB)

    def whole(t):
        return slice(t * PART, (t + 1) * PART)

    def live_rows(t, s):
        ids = lax.broadcasted_iota(I32, (SUB, LANE), 0)
        one = jnp.where(ids < live[0] - (t * PART + s * SUB), 1.0, 0.0)
        return jnp.concatenate([one] * (D // LANE), axis=1)

    def fwd_gather(t):
        rows = whole(t)
        z = dot(ohs[rows, :], table[0:TABLE, :]) + dot(ohr[rows, :], table[TABLE:WIDE, :])
        pre[rows, :] += z

    def fwd_silu(t):
        for s in range(SUBS):
            rows = part(t, s)
            h, slope = silu_parts(pre[rows, :])
            hid[rows, :] = h.astype(BF16)
            pre[rows, :] = slope

    def fwd_outer(t):
        post[t % 3] = dot(hid[whole(t), :], weo[...])

    def fwd_norm(t):
        for s in range(SUBS):
            rows = part(t, s)
            unit, inv = normalize(post[t % 3, s * SUB : (s + 1) * SUB, :] + eob[...])
            normed[rows, :] = unit.astype(BF16)
            scale[rows, :] = inv
            new = edges[rows, :].astype(F32) + unit * egain[...]
            prnd[rows, :] = (new * live_rows(t, s)).astype(BF16)

    def fwd_sum(t):
        got = dot(oht[TABLE:WIDE, whole(t)], prnd[whole(t), :])
        if t == 0:
            sum_acc[...] = got
        else:
            sum_acc[...] += got

    def at(f, t):
        if 0 <= t < PARTS:
            f(t)

    for t in range(PARTS + 3):
        at(fwd_gather, t)
        at(fwd_silu, t - 1)
        at(fwd_norm, t - 2)
        at(fwd_outer, t - 1)
        at(fwd_sum, t - 3)
    summed[...] = sum_acc[...].astype(BF16)

    def fold(x):
        return jnp.sum(x.reshape(x.shape[0] // 8, 8, x.shape[1]), axis=0)

    def half(t):
        return slice(t * NPART, (t + 1) * NPART)

    def strip(t, s):
        return slice(t * NPART + s * SUB, t * NPART + (s + 1) * SUB)

    halves = (0, 1)
    for t in halves:
        npre[half(t), :] += dot(summed[half(t), :], wni[D : 2 * D, :])
    for t in halves:
        for s in range(NSUBS):
            rows = strip(t, s)
            h, slope = silu_parts(npre[rows, :])
            nhid[rows, :] = h.astype(BF16)
            npre[rows, :] = slope
        npost[half(t), :] = dot(nhid[half(t), :], wno[...])
    for t in halves:
        for s in range(NSUBS):
            rows = strip(t, s)
            unit, inv = normalize(npost[rows, :] + nob[...])
            new_nodes[rows, :] = (nodes[rows, :].astype(F32) + unit * ngain[...]).astype(BF16)
            cotangent = cot[rows, :].astype(F32)
            acc[5] += fold(cotangent * unit)
            grad = norm_back(cotangent * ngain[...], unit, inv)
            acc[4] += fold(grad)
            npost_round[rows, :] = grad.astype(BF16)
        grad = dot_rt(npost_round[half(t), :], wno[...]) * npre[half(t), :]
        acc[3] += fold(grad)
        npre_round[half(t), :] = grad.astype(BF16)
    for t in halves:
        grad_rows[half(t), :] = dot_rt(npre_round[half(t), :], wni[D : 2 * D, :]).astype(BF16)
    s_nodes = store(0, new_nodes, new_nodes_h)

    def bwd_gather(t):
        post[t % 3] = dot(ohr[whole(t), :], grad_rows[...])

    def bwd_norm(t):
        for s in range(SUBS):
            rows = part(t, s)
            g = post[t % 3, s * SUB : (s + 1) * SUB, :] * live_rows(t, s)
            unit = normed[rows, :].astype(F32)
            acc[2] += fold(g * unit)
            grad = norm_back(g * egain[...], unit, scale[rows, :])
            acc[1] += fold(grad)
            prnd[rows, :] = grad.astype(BF16)

    def bwd_outer(t):
        got = dot_lt(hid[whole(t), :], prnd[whole(t), :])
        if t == 0:
            outer_acc[...] = got
        else:
            outer_acc[...] += got

    for t in range(PARTS + 2):
        at(bwd_gather, t)
        if t == 0:
            node_outer = dot_lt(nhid[...], npost_round[...])
            red_a.pack(2, node_outer)
            red_a.pack(0, dot_lt(nodes[...], npre_round[...]))
            red_a.pack(1, dot_lt(summed[...], npre_round[...]))
        at(bwd_norm, t - 1)
        if t == 1:
            red_a.step(0)
        if t == 2:
            node_base[...] = cot[...].astype(F32) + dot_rt(npre_round[...], wni[0:D, :])
        at(bwd_outer, t - 2)
    left, right = slice(0, D // 2), slice(D // 2, D)
    red_b.pack(3, outer_acc[:, left])
    red_b.pack(4, outer_acc[:, right])
    red_a.step(1)

    def bwd_inner(t, cols):
        grad = dot_rt(prnd[whole(t), :], weo[cols, :]) * pre[whole(t), cols]
        acc[0, :, cols] += fold(grad)
        prd[whole(t), cols] = grad.astype(BF16)

    def tall(red, cols):
        got = dot(oht[...], prd[:, cols])
        zb[:, cols] = got[0:WIDE].astype(BF16)
        red.pack(0, got[WIDE:TALL])

    def inner_sums(red, cols):
        incoming = halo_in[...].reshape(PEER, D)
        red.pack(1, dot_lt(nodes[...], zb[0:NODE, cols]) + dot_lt(incoming, zb[NODE:TABLE, cols]))
        red.pack(2, dot_lt(nodes[...], zb[TABLE:WIDE, cols]))
        red.step(0)

    for t in range(PARTS):
        bwd_inner(t, left)
    tall(red_b, left)
    for t in range(PARTS):
        bwd_inner(t, right)
    inner_sums(red_b, left)
    red_a.step(2)
    vec[0, 0:6, :] = jnp.sum(acc[...], axis=1)
    vec[0, 6:8, :] = jnp.zeros((2, D), F32)
    red_v.start(0)
    tall(red_c, right)
    red_b.step(1)
    inner_sums(red_c, right)
    red_a.step(3)
    red_v.finish(0)
    red_v.start(1)

    back = dot_rt(zb[NODE:TABLE, :], wei[D : 2 * D, :]).astype(BF16)
    back_out[...] = back.reshape(8, SLOT, D)
    returning = exchange(back_out, back_in, 8)
    red_c.step(1)
    red_a.step(4)
    stores = []

    def edge_out(c):
        rows = pl.ds(c * CHUNK, CHUNK)
        grad = dot_rt(prd[rows, 0:D], wei[0:D, :]) + dot(ohr[rows, :], grad_rows[...])
        alive = lax.broadcasted_iota(I32, (CHUNK, D), 0) < live[0] - c * CHUNK
        staging[rows, :] = jnp.where(alive, grad, 0.0).astype(BF16)
        stores.append(store(2 + c, staging.at[rows], edge_grad_h.at[rows]))

    edge_out(0)
    red_b.step(2)
    red_c.step(2)
    red_v.finish(1)
    red_v.start(2)
    red_a.step(5)
    edge_out(1)
    red_b.step(3)
    red_c.step(3)
    edge_out(2)
    red_b.step(4)
    red_c.step(4)
    red_v.finish(2)
    red_v.start(3)
    red_a.step(6)
    edge_out(3)
    red_b.step(5)
    red_c.step(5)
    node_base[...] += dot_rt(zb[0:NODE, :], wei[D : 2 * D, :])
    node_base[...] += dot_rt(zb[TABLE:WIDE, :], wei[2 * D : 3 * D, :])
    for c in returning:
        c.wait_recv()
    owned = dot(sendt[...], back_in[...].reshape(PEER, D))
    node_grad[...] = (node_base[...] + owned).astype(BF16)
    stores.append(store(1, node_grad, node_grad_h))
    red_v.finish(3)
    stores.append(store(6, vec.at[4], vec_h))
    red_a.step(7)
    stores.append(store(7, red_a.fin, fin_a_h))
    red_b.step(6)
    red_c.step(6)
    red_b.step(7)
    stores.append(store(8, red_b.fin, fin_b_h))
    red_c.step(7)
    stores.append(store(9, red_c.fin, fin_c_h))
    for c in halo + returning:
        c.wait_send()
    for red in (red_a, red_b, red_c, red_v):
        red.drain()
    s_nodes.wait()
    for c in stores:
        c.wait()


def fin_shape(nb, width):
    return (2, nb, 4, 4, 16, width)


FINS = ((3, D), (5, D // 2), (3, D // 2))


def reduce_bufs(nb, width):
    tile = (16, width)
    return (
        pltpu.VMEM(fin_shape(nb, width), BF16),
        pltpu.VMEM((nb, 4, 4) + tile, BF16),
        pltpu.VMEM((nb, 4, 4) + tile, BF16),
        pltpu.VMEM((3, nb, 4) + tile, BF16),
        pltpu.VMEM((nb, 4) + tile, BF16),
        pltpu.VMEM((3, nb) + tile, BF16),
        pltpu.VMEM((nb,) + tile, BF16),
        pltpu.VMEM((3, nb) + tile, BF16),
        pltpu.VMEM(fin_shape(nb, width), BF16),
    )


def sem_pair(n):
    return (pltpu.SemaphoreType.DMA((n,)), pltpu.SemaphoreType.DMA((n,)))


def widen(
    fa, fb, fc, vec, new_nodes, node_grad, edge_grad,
    new_nodes_o, node_grad_o, edge_grad_o, edge_inner, edge_outer, node_inner, node_outer,
    v0, v1, v2, v3, v4, v5,
    va, vb, vc, vn, vg, ve, wide, in_sem, out_sem,
):
    outs = []

    def load(k, src, dst):
        c = pltpu.make_async_copy(src, dst, in_sem.at[k])
        c.start()
        return c

    def store(k, src, dst):
        c = pltpu.make_async_copy(src, dst, out_sem.at[k])
        c.start()
        outs.append(c)

    c_a = [load(h, fa.at[h], va.at[h]) for h in range(2)]
    c_b = [load(2 + h, fb.at[h], vb.at[h]) for h in range(2)]
    c_c = [load(4 + h, fc.at[h], vc.at[h]) for h in range(2)]
    c_e = [load(7 + k, edge_grad.at[pl.ds(k * 512, 512)], ve.at[pl.ds(k * 512, 512)]) for k in range(4)]
    c_n = load(11, new_nodes, vn)
    c_g = load(12, node_grad, vg)
    k_out = 0
    HALF = NODE // 2

    places = ((node_inner, 0), (node_inner, 512), (node_outer, 0))
    for h in range(2):
        c_a[h].wait()
        for j, (out, first) in enumerate(places):
            rows = pl.ds(j * 512 + h * HALF, HALF)
            wide[rows, :] = va[h, j].reshape(HALF, D).astype(F32)
            store(k_out, wide.at[rows], out.at[pl.ds(first + h * HALF, HALF)])
            k_out += 1
    for h in range(2):
        c_b[h].wait()
        c_c[h].wait()
        for j in range(3):
            rows = pl.ds(1536 + j * 512 + h * HALF, HALF)
            wide[rows, 0:HALF] = vb[h, j].reshape(HALF, HALF).astype(F32)
            wide[rows, HALF:D] = vc[h, j].reshape(HALF, HALF).astype(F32)
            store(k_out, wide.at[rows], edge_inner.at[pl.ds(j * 512 + h * HALF, HALF)])
            k_out += 1
    for h in range(2):
        rows = pl.ds(3072 + h * HALF, HALF)
        for j in range(2):
            wide[rows, j * HALF : (j + 1) * HALF] = vb[h, 3 + j].reshape(HALF, HALF).astype(F32)
        store(k_out, wide.at[rows], edge_outer.at[pl.ds(h * HALF, HALF)])
        k_out += 1
    for k in range(4):
        c_e[k].wait()
        store(k_out, ve.at[pl.ds(k * 512, 512)], edge_grad_o.at[pl.ds(k * 512, 512)])
        k_out += 1
    c_n.wait()
    store(k_out, vn, new_nodes_o)
    c_g.wait()
    store(k_out + 1, vg, node_grad_o)
    for k, out in enumerate((v0, v1, v2, v3, v4, v5)):
        out[...] = vec[k : k + 1, :]
    for c in outs:
        c.wait()


def unpack(outs):
    new_nodes, node_grad, edge_grad, fa, fb, fc, vec = outs
    hbm = pl.BlockSpec(memory_space=pl.ANY)
    vm = pl.BlockSpec(memory_space=pltpu.VMEM)
    shapes = [
        ((NODE, D), BF16), ((NODE, D), BF16), ((EDGE, D), BF16),
        ((3 * D, D), F32), ((D, D), F32), ((2 * D, D), F32), ((D, D), F32),
    ] + [((1, D), F32)] * 6
    scratch = [pltpu.VMEM(fin_shape(*f), BF16) for f in FINS]
    return pl.pallas_call(
        widen,
        out_shape=[jax.ShapeDtypeStruct(s, t) for s, t in shapes],
        in_specs=[hbm] * 3 + [vm] + [hbm] * 3,
        out_specs=[hbm] * 7 + [vm] * 6,
        scratch_shapes=scratch + [
            pltpu.VMEM((NODE, D), BF16), pltpu.VMEM((NODE, D), BF16), pltpu.VMEM((EDGE, D), BF16),
            pltpu.VMEM((7 * D, D), F32),
            pltpu.SemaphoreType.DMA((13,)), pltpu.SemaphoreType.DMA((20,)),
        ],
        compiler_params=pltpu.CompilerParams(vmem_limit_bytes=63 * 2**20),
        name="widen",
    )(fa, fb, fc, vec, new_nodes, node_grad, edge_grad)


def body(
    node_states, edge_states, senders, receivers, live_count, send_rows, node_cotangent,
    edge_inner, edge_inbias, edge_outer, edge_outbias, edge_gain,
    node_inner, node_inbias, node_outer, node_outbias, node_gain,
):
    hbm = pl.BlockSpec(memory_space=pl.ANY)
    vm = pl.BlockSpec(memory_space=pltpu.VMEM)
    sm = pl.BlockSpec(memory_space=pltpu.SMEM)

    def row(v):
        return v.reshape(1, D)

    def v(shape, dtype=BF16):
        return pltpu.VMEM(shape, dtype)

    outs = pl.pallas_call(
        layer,
        out_shape=[
            jax.ShapeDtypeStruct((NODE, D), BF16),
            jax.ShapeDtypeStruct((NODE, D), BF16),
            jax.ShapeDtypeStruct((EDGE, D), BF16),
        ]
        + [jax.ShapeDtypeStruct(fin_shape(*f), BF16) for f in FINS]
        + [jax.ShapeDtypeStruct((8, D), F32)],
        in_specs=[
            hbm, hbm, vm, vm, sm, vm, hbm,
            hbm, vm, hbm, vm, vm, hbm, vm, hbm, vm, vm,
        ],
        out_specs=[hbm] * 7,
        scratch_shapes=[
            v((NODE, D)), v((EDGE, D)), v((NODE, D)),
            v((3 * D, D)), v((D, D)), v((2 * D, D)), v((D, D)),
            v((EDGE, TABLE)), v((TALL, EDGE)), v((EDGE, NODE)),
            v((EDGE, D), F32), v((EDGE, D)), v((EDGE, D)), v((EDGE, 1), F32),
            v((EDGE, D)), v((EDGE, D)), v((3, PART, D), F32),
            v((WIDE, D)), v((NODE, D)), v((WIDE, D)),
            v((8, SLOT, D)), v((8, SLOT, D)), v((8, SLOT, D)), v((8, SLOT, D)),
            v((NODE, PEER)),
            v((NODE, D)), v((NODE, D), F32), v((NODE, D)), v((NODE, D)),
            v((NODE, D), F32), v((D, D), F32),
            v((NODE, D), F32), v((NODE, D), F32), v((NODE, D)), v((NODE, D)), v((NODE, D)),
            v((6, 8, D), F32),
        ]
        + [reduce_bufs(*f) for f in FINS]
        + [
            v((5, 8, D), F32), v((10, 8, D), F32),
            pltpu.SemaphoreType.DMA((7,)), pltpu.SemaphoreType.DMA((11,)),
            pltpu.SemaphoreType.DMA((16,)), pltpu.SemaphoreType.DMA((16,)),
            sem_pair(47), sem_pair(47), sem_pair(47), sem_pair(10),
        ],
        compiler_params=pltpu.CompilerParams(
            collective_id=0, has_side_effects=True, vmem_limit_bytes=63 * 2**20
        ),
        name="layer",
    )(
        node_states, edge_states, senders.reshape(16, LANE), receivers.reshape(16, LANE),
        live_count, send_rows, node_cotangent,
        edge_inner, row(edge_inbias), edge_outer, row(edge_outbias), row(edge_gain),
        node_inner, row(node_inbias), node_outer, row(node_outbias), row(node_gain),
    )
    new_nodes, node_grad, edge_grad, ei, eo, ni, no, *vecs = unpack(outs)
    vecs = [x.reshape(D) for x in vecs]
    return (
        new_nodes, node_grad, edge_grad,
        ei, vecs[0], eo, vecs[1], vecs[2],
        ni, vecs[3], no, vecs[4], vecs[5],
    )


def solution(mesh):
    nodes = P(("lat", "lon"), None)
    flat = P(("lat", "lon"))
    return jax.shard_map(
        body,
        mesh=mesh,
        in_specs=(nodes, nodes, flat, flat, flat, nodes, nodes) + (P(),) * 10,
        out_specs=(nodes, nodes, nodes) + (P(),) * 10,
        check_vma=False,
    )
```

```python
import functools

import jax
import jax.numpy as jnp
from jax import lax
from jax.experimental import pallas as pl
from jax.experimental.pallas import tpu as pltpu
from jax.sharding import PartitionSpec as P

MESH = pl.DeviceIdType.MESH
F32 = jnp.float32
BF16 = jnp.bfloat16
I32 = jnp.int32
epsilon = 1e-05

D = 512
NODE = 512
EDGE = 2048
SLOT = 32
PEER = 256
TABLE = NODE + PEER
WIDE = TABLE + NODE
CHUNK = 512
STEPS = EDGE // CHUNK
PART = 512
NPART = 256
NSUBS = NPART // 32
TALL = NODE + PEER + NODE + D
PARTS = EDGE // PART
SUB = 32
SUBS = PART // SUB
LANE = 128
N_LAT = 8
N_LON = 16
OFFSETS = ((-1, -1), (-1, 0), (-1, 1), (0, -1), (0, 1), (1, -1), (1, 0), (1, 1))


def dot(a, b):
    return jnp.dot(a, b, preferred_element_type=F32)


def dot_rt(a, b):
    return lax.dot_general(a, b, (((1,), (1,)), ((), ())), preferred_element_type=F32)


def dot_lt(a, b):
    return lax.dot_general(a, b, (((0,), (0,)), ((), ())), preferred_element_type=F32)


def row_mean(x):
    return jnp.sum(x, axis=-1, keepdims=True) * (1.0 / D)


def col_sum(x):
    return jnp.sum(x, axis=0, keepdims=True)


def silu_parts(z):
    sig = 0.5 + 0.5 * jnp.tanh(0.5 * z)
    h = z * sig
    return h, sig + h * (1.0 - sig)


def normalize(post):
    centered = post - row_mean(post)
    scale = lax.rsqrt(row_mean(centered * centered) + epsilon)
    return centered * scale, scale


def norm_back(t, normed, scale):
    return scale * (t - row_mean(t) - normed * row_mean(t * normed))


def column_of(row):
    return jnp.transpose(jnp.broadcast_to(row.astype(F32), (LANE, LANE))).astype(I32)


def lanes(base):
    return lax.broadcasted_iota(I32, (LANE, LANE), 1) + base


def hot(mask):
    return jnp.where(mask, 1.0, 0.0).astype(BF16)


class Place:
    def __init__(self):
        self.lat = lax.axis_index("lat")
        self.lon = lax.axis_index("lon")
        self.core = lax.rem(self.lat, 2)
        self.y = lax.div(self.lat, 2)
        self.x = lax.div(self.lon, 4)
        self.z = lax.rem(self.lon, 4)

    def neighbour(self, n):
        dlat, dlon = OFFSETS[n]
        return (
            lax.rem(self.lat + (dlat + N_LAT), N_LAT),
            lax.rem(self.lon + (dlon + N_LON), N_LON),
        )

    def twin(self):
        return (self.y * 2 + (1 - self.core), self.lon)

    def index(self, axis):
        is_x = lax.div((2 - axis) * (1 - axis), 2)
        is_y = axis * (2 - axis)
        is_z = lax.div(axis * (axis - 1), 2)
        return self.x * is_x + self.y * is_y + self.z * is_z

    def shifted(self, axis, d):
        is_x = lax.div((2 - axis) * (1 - axis), 2)
        is_y = axis * (2 - axis)
        is_z = lax.div(axis * (axis - 1), 2)
        x = lax.rem(self.x + d * is_x, 4)
        y = lax.rem(self.y + d * is_y, 4)
        z = lax.rem(self.z + d * is_z, 4)
        return (y * 2 + self.core, x * 4 + z)

    def axis(self, b, level):
        return lax.rem(self.core + (b + level), 3)


class Reduce:
    def __init__(self, place, streams, gb, rc, s0, q1, t1, r1, s1, r2, s2, r3, fin, send, recv):
        self.p, self.streams = place, streams
        self.gb, self.rc, self.s0, self.q1, self.t1 = gb, rc, s0, q1, t1
        self.r1, self.s1, self.r2, self.s2, self.r3, self.fin = r1, s1, r2, s2, r3, fin
        self.send, self.recv = send, recv
        self.copies = {}
        self.used = 0

    def pack(self, j, val):
        width = val.shape[1]
        self.gb[:, j] = val.astype(BF16).reshape(2, 4, 4, 16, width)

    def copy(self, step, src, dst, device):
        c = pltpu.make_async_remote_copy(
            src_ref=src,
            dst_ref=dst,
            send_sem=self.send.at[self.used],
            recv_sem=self.recv.at[self.used],
            device_id=device,
            device_id_type=MESH,
        )
        c.start()
        self.used += 1
        self.copies.setdefault(step, []).append(c)

    def wait(self, step):
        for c in self.copies[step]:
            c.wait_recv()

    def spread(self, step, level, src, dst):
        for n, part in enumerate(self.streams):
            axis = self.p.axis(n, level)
            for d in (2, 1, 3):
                there = lax.rem(self.p.index(axis) + d, 4)
                self.copy(step, src(n, part, there), dst(n, part, d), self.p.shifted(axis, d))

    def step(self, k):
        h = self.p.core
        count = len(self.streams)
        ring = [self.p.axis(n, 0) for n in range(count)]
        own = [self.p.index(axis) for axis in ring]
        ahead = [[lax.rem(i + d, 4) for d in range(4)] for i in own]
        own2 = [self.p.index(self.p.axis(n, 1)) for n in range(count)]
        low, high = slice(0, 2), slice(2, 4)
        if k == 0:
            self.copy(0, self.gb.at[1 - h], self.rc, self.p.twin())
        elif k == 1:
            self.wait(0)
            for part in self.streams:
                mine = self.gb[h, part].astype(F32)
                self.s0[part] = (mine + self.rc[part].astype(F32)).astype(BF16)
            for n, part in enumerate(self.streams):
                up, down = self.p.shifted(ring[n], 1), self.p.shifted(ring[n], 3)
                _, one, two, three = ahead[n]
                self.copy("up", self.s0.at[part, two, low], self.q1.at[0, part], up)
                self.copy("down", self.s0.at[part, two, high], self.q1.at[1, part], down)
                self.copy(1, self.s0.at[part, one, high], self.r1.at[0, part], up)
                self.copy(1, self.s0.at[part, three, low], self.r1.at[1, part], down)
        elif k == 2:
            self.wait("up")
            self.wait("down")
            for n, part in enumerate(self.streams):
                up, down = self.p.shifted(ring[n], 1), self.p.shifted(ring[n], 3)
                _, one, _, three = ahead[n]
                mine = self.s0[part, one, low].astype(F32)
                self.t1[0, part] = (mine + self.q1[0, part].astype(F32)).astype(BF16)
                mine = self.s0[part, three, high].astype(F32)
                self.t1[1, part] = (mine + self.q1[1, part].astype(F32)).astype(BF16)
                self.copy(1, self.t1.at[0, part], self.r1.at[2, part], up)
                self.copy(1, self.t1.at[1, part], self.r1.at[3, part], down)
        elif k == 3:
            self.wait(1)
            for n, part in enumerate(self.streams):
                for cut, first, second in ((low, 1, 2), (high, 0, 3)):
                    total = self.s0[part, own[n], cut].astype(F32)
                    total += self.r1[first, part].astype(F32)
                    total += self.r1[second, part].astype(F32)
                    self.s1[part, cut] = total.astype(BF16)
            self.spread(
                2, 1, lambda n, part, i: self.s1.at[part, i], lambda n, part, d: self.r2.at[d - 1, part]
            )
        elif k == 4:
            self.wait(2)
            for n, part in enumerate(self.streams):
                total = self.s1[part, own2[n]].astype(F32)
                for d in range(3):
                    total += self.r2[d, part].astype(F32)
                self.s2[part] = total.astype(BF16)
            self.spread(
                3, 2, lambda n, part, i: self.s2.at[part], lambda n, part, d: self.r3.at[d - 1, part]
            )
        elif k == 5:
            self.wait(3)
            for n, part in enumerate(self.streams):
                near = self.s2[part].astype(F32) + self.r3[1, part].astype(F32)
                far = self.r3[0, part].astype(F32) + self.r3[2, part].astype(F32)
                self.fin[h, part, own[n], own2[n]] = (near + far).astype(BF16)

            def piece(n, part, _):
                return self.fin.at[h, part, own[n], own2[n]]

            self.spread(4, 1, piece, piece)
        elif k == 6:
            self.wait(4)
            for n, part in enumerate(self.streams):
                piece = self.fin.at[h, part, own[n]]
                self.copy(5, piece, piece, self.p.shifted(ring[n], 1))
                self.copy(5, piece, piece, self.p.shifted(ring[n], 3))
        elif k == 7:
            self.wait(5)
            for n, part in enumerate(self.streams):
                _, one, _, three = ahead[n]
                piece = self.fin.at[h, part, three, low]
                self.copy(6, piece, piece, self.p.shifted(ring[n], 1))
                piece = self.fin.at[h, part, one, high]
                self.copy(6, piece, piece, self.p.shifted(ring[n], 3))
        elif k == 8:
            self.wait(6)
            self.copy(7, self.fin.at[h], self.fin.at[h], self.p.twin())
        elif k == 9:
            self.wait(7)

    def drain(self):
        for group in self.copies.values():
            for c in group:
                c.wait_send()


class Vectors:
    def __init__(self, place, val, slots, send, recv):
        self.p, self.val, self.slots, self.send, self.recv = place, val, slots, send, recv
        self.copies = []

    def start(self, k):
        axis = k - 1
        hops = ((0, self.p.twin()),) if k == 0 else tuple(
            (d, self.p.shifted(jnp.int32(axis), d)) for d in (1, 2, 3)
        )
        for d, device in hops:
            at = 0 if k == 0 else 3 * (k - 1) + d
            c = pltpu.make_async_remote_copy(
                src_ref=self.val.at[k],
                dst_ref=self.slots.at[at],
                send_sem=self.send.at[at],
                recv_sem=self.recv.at[at],
                device_id=device,
                device_id_type=MESH,
            )
            c.start()
            self.copies.append((k, c))

    def finish(self, k):
        for j, c in self.copies:
            if j == k:
                c.wait_recv()
        if k == 0:
            self.val[1] = self.val[0] + self.slots[0]
        else:
            at = 3 * (k - 1)
            near = self.val[k] + self.slots[at + 2]
            far = self.slots[at + 1] + self.slots[at + 3]
            self.val[k + 1] = near + far

    def drain(self):
        for _, c in self.copies:
            c.wait_send()


def layer(
    nodes_h, edges_h, senders, receivers, live, send_rows, cot_h,
    wei_h, eib, weo_h, eob, egain, wni_h, nib, wno_h, nob, ngain,
    new_nodes_h, node_grad_h, edge_grad_h, fin_a_h, fin_b_h, fin_c_h, vec_h,
    nodes, edges, cot, wei, weo, wni, wno,
    ohs, oht, ohr, pre, hid, normed, scale, prnd, staging, post,
    table, grad_rows, zb, halo_out, halo_in, back_out, back_in, sendt,
    new_nodes, node_base, node_grad, summed, sum_acc, outer_acc,
    npre, npost, nhid, npost_round, npre_round, acc,
    bufs_a, bufs_b, bufs_c, vec, vec_slots,
    in_sem, out_sem, halo_send, halo_recv, sems_a, sems_b, sems_c, sems_v,
):
    place = Place()
    prd = ohs

    def load(k, src, dst):
        c = pltpu.make_async_copy(src, dst, in_sem.at[k])
        c.start()
        return c

    def store(k, src, dst):
        c = pltpu.make_async_copy(src, dst, out_sem.at[k])
        c.start()
        return c

    c_nodes = load(0, nodes_h, nodes)
    c_wei = load(1, wei_h, wei)
    c_edges = load(2, edges_h, edges)
    c_wni = load(4, wni_h, wni)
    c_weo = load(3, weo_h, weo)
    c_wno = load(5, wno_h, wno)
    c_cot = load(6, cot_h, cot)

    barrier = pltpu.get_barrier_semaphore()
    partners = [place.neighbour(n) for n in range(8)] + [place.twin()]
    for axis in range(3):
        for d in (1, 2, 3):
            partners.append(place.shifted(jnp.int32(axis), d))
    for device in partners:
        pl.semaphore_signal(barrier, inc=1, device_id=device, device_id_type=MESH)

    thirds = (slice(0, 1), slice(1, 2), slice(2, 3))
    red_a = Reduce(place, thirds, *bufs_a, *sems_a)
    red_b = Reduce(place, (slice(0, 2), slice(2, 4), slice(4, 5)), *bufs_b, *sems_b)
    red_c = Reduce(place, thirds, *bufs_c, *sems_c)
    red_v = Vectors(place, vec, vec_slots, *sems_v)

    picks = []
    for k in range(2):
        col = column_of(send_rows[:, k * LANE : (k + 1) * LANE])
        picks.append(jnp.concatenate([hot(col == lanes(j * LANE)) for j in range(4)], axis=1))
    picks = jnp.concatenate(picks, axis=0)
    c_nodes.wait()
    halo_out[...] = dot(picks, nodes[...]).astype(BF16).reshape(8, SLOT, D)
    pl.semaphore_wait(barrier, len(partners))

    def exchange(src, dst, base):
        copies = []
        for n in range(8):
            c = pltpu.make_async_remote_copy(
                src_ref=src.at[n],
                dst_ref=dst.at[7 - n],
                send_sem=halo_send.at[base + n],
                recv_sem=halo_recv.at[base + 7 - n],
                device_id=place.neighbour(n),
                device_id_type=MESH,
            )
            c.start()
            copies.append(c)
        return copies

    halo = exchange(halo_out, halo_in, 0)

    rowi = lax.broadcasted_iota(I32, (NODE, LANE), 0)
    for k in range(2):
        row = send_rows[:, k * LANE : (k + 1) * LANE]
        sendt[:, k * LANE : (k + 1) * LANE] = hot(rowi == row)
    acc[...] = jnp.zeros_like(acc)
    c_wei.wait()
    table[0:NODE, :] = dot(nodes[...], wei[D : 2 * D, :]).astype(BF16)
    table[TABLE:WIDE, :] = dot(nodes[...], wei[2 * D : 3 * D, :]).astype(BF16)
    c_edges.wait()

    def early(c):
        rows = slice(c * CHUNK, (c + 1) * CHUNK)
        pre[rows, :] = dot(edges[rows, :], wei[0:D, :]) + eib[...]
        for j in range(c * (CHUNK // LANE), (c + 1) * (CHUNK // LANE)):
            s_col, r_col = column_of(senders[j : j + 1, :]), column_of(receivers[j : j + 1, :])
            here = slice(j * LANE, (j + 1) * LANE)
            for k in range(TABLE // LANE):
                ohs[here, k * LANE : (k + 1) * LANE] = hot(s_col == lanes(k * LANE))
            for k in range(NODE // LANE):
                ohr[here, k * LANE : (k + 1) * LANE] = hot(r_col == lanes(k * LANE))
            oht[TABLE:WIDE, here] = hot(rowi == receivers[j : j + 1, :])

    def late(c):
        rows = slice(c * CHUNK, (c + 1) * CHUNK)
        oht[WIDE:TALL, rows] = jnp.transpose(edges[rows, :])
        ids = lax.broadcasted_iota(I32, (TABLE, LANE), 0)
        for j in range(c * (CHUNK // LANE), (c + 1) * (CHUNK // LANE)):
            oht[0:TABLE, j * LANE : (j + 1) * LANE] = hot(ids == senders[j : j + 1, :])

    for c in range(STEPS):
        early(c)
    c_wni.wait()
    npre[...] = dot(nodes[...], wni[0:D, :]) + nib[...]
    c_weo.wait()
    c_wno.wait()
    c_cot.wait()

    for c in halo:
        c.wait_recv()
    table[NODE:TABLE, :] = dot(halo_in[...].reshape(PEER, D), wei[D : 2 * D, :]).astype(BF16)

    def part(t, s):
        return slice(t * PART + s * SUB, t * PART + (s + 1) * SUB)

    def whole(t):
        return slice(t * PART, (t + 1) * PART)

    def live_rows(t, s):
        ids = lax.broadcasted_iota(I32, (SUB, LANE), 0)
        one = jnp.where(ids < live[0] - (t * PART + s * SUB), 1.0, 0.0)
        return jnp.concatenate([one] * (D // LANE), axis=1)

    def fwd_gather(t):
        rows = whole(t)
        z = dot(ohs[rows, :], table[0:TABLE, :]) + dot(ohr[rows, :], table[TABLE:WIDE, :])
        pre[rows, :] += z

    def fwd_silu(t):
        for s in range(SUBS):
            rows = part(t, s)
            h, slope = silu_parts(pre[rows, :])
            hid[rows, :] = h.astype(BF16)
            pre[rows, :] = slope

    def fwd_outer(t):
        post[t % 3] = dot(hid[whole(t), :], weo[...])

    def fwd_norm(t):
        for s in range(SUBS):
            rows = part(t, s)
            unit, inv = normalize(post[t % 3, s * SUB : (s + 1) * SUB, :] + eob[...])
            normed[rows, :] = unit.astype(BF16)
            scale[rows, :] = inv
            new = edges[rows, :].astype(F32) + unit * egain[...]
            prnd[rows, :] = (new * live_rows(t, s)).astype(BF16)

    def fwd_sum(t):
        got = dot(oht[TABLE:WIDE, whole(t)], prnd[whole(t), :])
        if t == 0:
            sum_acc[...] = got
        else:
            sum_acc[...] += got

    def at(f, t):
        if 0 <= t < PARTS:
            f(t)

    for t in range(PARTS + 3):
        at(fwd_gather, t)
        at(fwd_silu, t - 1)
        at(fwd_norm, t - 2)
        at(fwd_outer, t - 1)
        at(fwd_sum, t - 3)
    summed[...] = sum_acc[...].astype(BF16)

    def fold(x):
        return jnp.sum(x.reshape(x.shape[0] // 8, 8, x.shape[1]), axis=0)

    def half(t):
        return slice(t * NPART, (t + 1) * NPART)

    def strip(t, s):
        return slice(t * NPART + s * SUB, t * NPART + (s + 1) * SUB)

    halves = (0, 1)
    for t in halves:
        npre[half(t), :] += dot(summed[half(t), :], wni[D : 2 * D, :])
        late(t)
    for t in halves:
        for s in range(NSUBS):
            rows = strip(t, s)
            h, slope = silu_parts(npre[rows, :])
            nhid[rows, :] = h.astype(BF16)
            npre[rows, :] = slope
        npost[half(t), :] = dot(nhid[half(t), :], wno[...])
    for t in halves:
        for s in range(NSUBS):
            rows = strip(t, s)
            unit, inv = normalize(npost[rows, :] + nob[...])
            new_nodes[rows, :] = (nodes[rows, :].astype(F32) + unit * ngain[...]).astype(BF16)
            cotangent = cot[rows, :].astype(F32)
            acc[5] += fold(cotangent * unit)
            grad = norm_back(cotangent * ngain[...], unit, inv)
            acc[4] += fold(grad)
            npost_round[rows, :] = grad.astype(BF16)
        grad = dot_rt(npost_round[half(t), :], wno[...]) * npre[half(t), :]
        acc[3] += fold(grad)
        npre_round[half(t), :] = grad.astype(BF16)
        late(2 + t)
    for t in halves:
        grad_rows[half(t), :] = dot_rt(npre_round[half(t), :], wni[D : 2 * D, :]).astype(BF16)
    s_nodes = store(0, new_nodes, new_nodes_h)

    def bwd_gather(t):
        post[t % 3] = dot(ohr[whole(t), :], grad_rows[...])

    def bwd_norm(t):
        for s in range(SUBS):
            rows = part(t, s)
            g = post[t % 3, s * SUB : (s + 1) * SUB, :] * live_rows(t, s)
            unit = normed[rows, :].astype(F32)
            acc[2] += fold(g * unit)
            grad = norm_back(g * egain[...], unit, scale[rows, :])
            acc[1] += fold(grad)
            prnd[rows, :] = grad.astype(BF16)

    def bwd_outer(t):
        got = dot_lt(hid[whole(t), :], prnd[whole(t), :])
        if t == 0:
            outer_acc[...] = got
        else:
            outer_acc[...] += got

    for t in range(PARTS + 2):
        at(bwd_gather, t)
        if t == 0:
            red_a.pack(2, dot_lt(nhid[...], npost_round[...]))
            red_a.pack(0, dot_lt(nodes[...], npre_round[...]))
            red_a.pack(1, dot_lt(summed[...], npre_round[...]))
        at(bwd_norm, t - 1)
        if t == 1:
            red_a.step(0)
        if t == 2:
            node_base[...] = cot[...].astype(F32) + dot_rt(npre_round[...], wni[0:D, :])
        if t == 3:
            red_a.step(1)
        at(bwd_outer, t - 2)
    left, right = slice(0, D // 2), slice(D // 2, D)
    red_b.pack(3, outer_acc[:, left])
    red_b.pack(4, outer_acc[:, right])
    red_a.step(2)

    def bwd_inner(t, cols):
        grad = dot_rt(prnd[whole(t), :], weo[cols, :]) * pre[whole(t), cols]
        acc[0, :, cols] += fold(grad)
        prd[whole(t), cols] = grad.astype(BF16)

    def tall(red, cols):
        got = dot(oht[...], prd[:, cols])
        zb[:, cols] = got[0:WIDE].astype(BF16)
        red.pack(0, got[WIDE:TALL])

    def inner_sums(red, cols):
        incoming = halo_in[...].reshape(PEER, D)
        red.pack(1, dot_lt(nodes[...], zb[0:NODE, cols]) + dot_lt(incoming, zb[NODE:TABLE, cols]))
        red.pack(2, dot_lt(nodes[...], zb[TABLE:WIDE, cols]))
        red.step(0)

    for t in range(PARTS):
        bwd_inner(t, left)
    red_a.step(3)
    tall(red_b, left)
    for t in range(PARTS):
        bwd_inner(t, right)
    red_a.step(4)
    inner_sums(red_b, left)
    vec[0, 0:6, :] = jnp.sum(acc[...], axis=1)
    vec[0, 6:8, :] = jnp.zeros((2, D), F32)
    red_v.start(0)
    red_a.step(5)
    tall(red_c, right)
    red_b.step(1)
    inner_sums(red_c, right)
    red_a.step(6)
    red_b.step(2)
    red_v.finish(0)
    red_v.start(1)

    back = dot_rt(zb[NODE:TABLE, :], wei[D : 2 * D, :]).astype(BF16)
    back_out[...] = back.reshape(8, SLOT, D)
    returning = exchange(back_out, back_in, 8)
    red_c.step(1)
    red_b.step(3)
    stores = []

    def edge_out(c):
        rows = pl.ds(c * CHUNK, CHUNK)
        grad = dot_rt(prd[rows, 0:D], wei[0:D, :]) + dot(ohr[rows, :], grad_rows[...])
        alive = lax.broadcasted_iota(I32, (CHUNK, D), 0) < live[0] - c * CHUNK
        staging[rows, :] = jnp.where(alive, grad, 0.0).astype(BF16)
        stores.append(store(2 + c, staging.at[rows], edge_grad_h.at[rows]))

    edge_out(0)
    red_c.step(2)
    red_a.step(7)
    red_b.step(4)
    red_v.finish(1)
    red_v.start(2)
    edge_out(1)
    red_c.step(3)
    red_b.step(5)
    red_a.step(8)
    edge_out(2)
    red_c.step(4)
    red_b.step(6)
    red_v.finish(2)
    red_v.start(3)
    edge_out(3)
    red_c.step(5)
    red_b.step(7)
    node_base[...] += dot_rt(zb[0:NODE, :], wei[D : 2 * D, :])
    node_base[...] += dot_rt(zb[TABLE:WIDE, :], wei[2 * D : 3 * D, :])
    red_c.step(6)
    for c in returning:
        c.wait_recv()
    owned = dot(sendt[...], back_in[...].reshape(PEER, D))
    node_grad[...] = (node_base[...] + owned).astype(BF16)
    stores.append(store(1, node_grad, node_grad_h))
    red_v.finish(3)
    stores.append(store(6, vec.at[4], vec_h))
    red_b.step(8)
    red_a.step(9)
    stores.append(store(7, red_a.fin, fin_a_h))
    red_c.step(7)
    red_b.step(9)
    stores.append(store(8, red_b.fin, fin_b_h))
    red_c.step(8)
    red_c.step(9)
    stores.append(store(9, red_c.fin, fin_c_h))
    for c in halo + returning:
        c.wait_send()
    for red in (red_a, red_b, red_c, red_v):
        red.drain()
    s_nodes.wait()
    for c in stores:
        c.wait()


def fin_shape(nb, width):
    return (2, nb, 4, 4, 16, width)


FINS = ((3, D), (5, D // 2), (3, D // 2))


def reduce_bufs(nb, width):
    tile = (16, width)
    return (
        pltpu.VMEM(fin_shape(nb, width), BF16),
        pltpu.VMEM((nb, 4, 4) + tile, BF16),
        pltpu.VMEM((nb, 4, 4) + tile, BF16),
        pltpu.VMEM((2, nb, 2) + tile, BF16),
        pltpu.VMEM((2, nb, 2) + tile, BF16),
        pltpu.VMEM((4, nb, 2) + tile, BF16),
        pltpu.VMEM((nb, 4) + tile, BF16),
        pltpu.VMEM((3, nb) + tile, BF16),
        pltpu.VMEM((nb,) + tile, BF16),
        pltpu.VMEM((3, nb) + tile, BF16),
        pltpu.VMEM(fin_shape(nb, width), BF16),
    )


def sem_pair(n):
    return (pltpu.SemaphoreType.DMA((n,)), pltpu.SemaphoreType.DMA((n,)))


def widen(
    fa, fb, fc, vec, new_nodes, node_grad, edge_grad,
    new_nodes_o, node_grad_o, edge_grad_o, edge_inner, edge_outer, node_inner, node_outer,
    v0, v1, v2, v3, v4, v5,
    va, vb, vc, vn, vg, ve, wide, in_sem, out_sem,
):
    outs = []

    def load(k, src, dst):
        c = pltpu.make_async_copy(src, dst, in_sem.at[k])
        c.start()
        return c

    def store(k, src, dst):
        c = pltpu.make_async_copy(src, dst, out_sem.at[k])
        c.start()
        outs.append(c)

    c_a = [load(h, fa.at[h], va.at[h]) for h in range(2)]
    c_b = [load(2 + h, fb.at[h], vb.at[h]) for h in range(2)]
    c_c = [load(4 + h, fc.at[h], vc.at[h]) for h in range(2)]
    c_e = [load(7 + k, edge_grad.at[pl.ds(k * 512, 512)], ve.at[pl.ds(k * 512, 512)]) for k in range(4)]
    c_n = load(11, new_nodes, vn)
    c_g = load(12, node_grad, vg)
    k_out = 0
    HALF = NODE // 2

    places = ((node_inner, 0), (node_inner, 512), (node_outer, 0))
    for h in range(2):
        c_a[h].wait()
        for j, (out, first) in enumerate(places):
            rows = pl.ds(j * 512 + h * HALF, HALF)
            wide[rows, :] = va[h, j].reshape(HALF, D).astype(F32)
            store(k_out, wide.at[rows], out.at[pl.ds(first + h * HALF, HALF)])
            k_out += 1
    for h in range(2):
        c_b[h].wait()
        c_c[h].wait()
        for j in range(3):
            rows = pl.ds(1536 + j * 512 + h * HALF, HALF)
            wide[rows, 0:HALF] = vb[h, j].reshape(HALF, HALF).astype(F32)
            wide[rows, HALF:D] = vc[h, j].reshape(HALF, HALF).astype(F32)
            store(k_out, wide.at[rows], edge_inner.at[pl.ds(j * 512 + h * HALF, HALF)])
            k_out += 1
    for h in range(2):
        rows = pl.ds(3072 + h * HALF, HALF)
        for j in range(2):
            wide[rows, j * HALF : (j + 1) * HALF] = vb[h, 3 + j].reshape(HALF, HALF).astype(F32)
        store(k_out, wide.at[rows], edge_outer.at[pl.ds(h * HALF, HALF)])
        k_out += 1
    for k in range(4):
        c_e[k].wait()
        store(k_out, ve.at[pl.ds(k * 512, 512)], edge_grad_o.at[pl.ds(k * 512, 512)])
        k_out += 1
    c_n.wait()
    store(k_out, vn, new_nodes_o)
    c_g.wait()
    store(k_out + 1, vg, node_grad_o)
    for k, out in enumerate((v0, v1, v2, v3, v4, v5)):
        out[...] = vec[k : k + 1, :]
    for c in outs:
        c.wait()


def unpack(outs):
    new_nodes, node_grad, edge_grad, fa, fb, fc, vec = outs
    hbm = pl.BlockSpec(memory_space=pl.ANY)
    vm = pl.BlockSpec(memory_space=pltpu.VMEM)
    shapes = [
        ((NODE, D), BF16), ((NODE, D), BF16), ((EDGE, D), BF16),
        ((3 * D, D), F32), ((D, D), F32), ((2 * D, D), F32), ((D, D), F32),
    ] + [((1, D), F32)] * 6
    scratch = [pltpu.VMEM(fin_shape(*f), BF16) for f in FINS]
    return pl.pallas_call(
        widen,
        out_shape=[jax.ShapeDtypeStruct(s, t) for s, t in shapes],
        in_specs=[hbm] * 3 + [vm] + [hbm] * 3,
        out_specs=[hbm] * 7 + [vm] * 6,
        scratch_shapes=scratch + [
            pltpu.VMEM((NODE, D), BF16), pltpu.VMEM((NODE, D), BF16), pltpu.VMEM((EDGE, D), BF16),
            pltpu.VMEM((7 * D, D), F32),
            pltpu.SemaphoreType.DMA((13,)), pltpu.SemaphoreType.DMA((20,)),
        ],
        compiler_params=pltpu.CompilerParams(vmem_limit_bytes=63 * 2**20),
        name="widen",
    )(fa, fb, fc, vec, new_nodes, node_grad, edge_grad)


def body(
    node_states, edge_states, senders, receivers, live_count, send_rows, node_cotangent,
    edge_inner, edge_inbias, edge_outer, edge_outbias, edge_gain,
    node_inner, node_inbias, node_outer, node_outbias, node_gain,
):
    hbm = pl.BlockSpec(memory_space=pl.ANY)
    vm = pl.BlockSpec(memory_space=pltpu.VMEM)
    sm = pl.BlockSpec(memory_space=pltpu.SMEM)

    def row(v):
        return v.reshape(1, D)

    def v(shape, dtype=BF16):
        return pltpu.VMEM(shape, dtype)

    outs = pl.pallas_call(
        layer,
        out_shape=[
            jax.ShapeDtypeStruct((NODE, D), BF16),
            jax.ShapeDtypeStruct((NODE, D), BF16),
            jax.ShapeDtypeStruct((EDGE, D), BF16),
        ]
        + [jax.ShapeDtypeStruct(fin_shape(*f), BF16) for f in FINS]
        + [jax.ShapeDtypeStruct((8, D), F32)],
        in_specs=[
            hbm, hbm, vm, vm, sm, vm, hbm,
            hbm, vm, hbm, vm, vm, hbm, vm, hbm, vm, vm,
        ],
        out_specs=[hbm] * 7,
        scratch_shapes=[
            v((NODE, D)), v((EDGE, D)), v((NODE, D)),
            v((3 * D, D)), v((D, D)), v((2 * D, D)), v((D, D)),
            v((EDGE, TABLE)), v((TALL, EDGE)), v((EDGE, NODE)),
            v((EDGE, D), F32), v((EDGE, D)), v((EDGE, D)), v((EDGE, 1), F32),
            v((EDGE, D)), v((EDGE, D)), v((3, PART, D), F32),
            v((WIDE, D)), v((NODE, D)), v((WIDE, D)),
            v((8, SLOT, D)), v((8, SLOT, D)), v((8, SLOT, D)), v((8, SLOT, D)),
            v((NODE, PEER)),
            v((NODE, D)), v((NODE, D), F32), v((NODE, D)), v((NODE, D)),
            v((NODE, D), F32), v((D, D), F32),
            v((NODE, D), F32), v((NODE, D), F32), v((NODE, D)), v((NODE, D)), v((NODE, D)),
            v((6, 8, D), F32),
        ]
        + [reduce_bufs(*f) for f in FINS]
        + [
            v((5, 8, D), F32), v((10, 8, D), F32),
            pltpu.SemaphoreType.DMA((7,)), pltpu.SemaphoreType.DMA((11,)),
            pltpu.SemaphoreType.DMA((16,)), pltpu.SemaphoreType.DMA((16,)),
            sem_pair(59), sem_pair(59), sem_pair(59), sem_pair(10),
        ],
        compiler_params=pltpu.CompilerParams(
            collective_id=0, has_side_effects=True, vmem_limit_bytes=63 * 2**20
        ),
        name="layer",
    )(
        node_states, edge_states, senders.reshape(16, LANE), receivers.reshape(16, LANE),
        live_count, send_rows, node_cotangent,
        edge_inner, row(edge_inbias), edge_outer, row(edge_outbias), row(edge_gain),
        node_inner, row(node_inbias), node_outer, row(node_outbias), row(node_gain),
    )
    new_nodes, node_grad, edge_grad, ei, eo, ni, no, *vecs = unpack(outs)
    vecs = [x.reshape(D) for x in vecs]
    return (
        new_nodes, node_grad, edge_grad,
        ei, vecs[0], eo, vecs[1], vecs[2],
        ni, vecs[3], no, vecs[4], vecs[5],
    )


def solution(mesh):
    nodes = P(("lat", "lon"), None)
    flat = P(("lat", "lon"))
    return jax.shard_map(
        body,
        mesh=mesh,
        in_specs=(nodes, nodes, flat, flat, flat, nodes, nodes) + (P(),) * 10,
        out_specs=(nodes, nodes, nodes) + (P(),) * 10,
        check_vma=False,
    )
```

```python
import functools

import jax
import jax.numpy as jnp
from jax import lax
from jax.experimental import pallas as pl
from jax.experimental.pallas import tpu as pltpu
from jax.sharding import PartitionSpec as P

MESH = pl.DeviceIdType.MESH
F32 = jnp.float32
BF16 = jnp.bfloat16
I32 = jnp.int32
epsilon = 1e-05

D = 512
NODE = 512
EDGE = 2048
SLOT = 32
PEER = 256
TABLE = NODE + PEER
WIDE = TABLE + NODE
CHUNK = 512
STEPS = EDGE // CHUNK
PART = 512
NPART = 256
NSUBS = NPART // 32
TALL = NODE + PEER + NODE + D
PARTS = EDGE // PART
SUB = 32
SUBS = PART // SUB
LANE = 128
N_LAT = 8
N_LON = 16
OFFSETS = ((-1, -1), (-1, 0), (-1, 1), (0, -1), (0, 1), (1, -1), (1, 0), (1, 1))


def dot(a, b):
    return jnp.dot(a, b, preferred_element_type=F32)


def dot_rt(a, b):
    return lax.dot_general(a, b, (((1,), (1,)), ((), ())), preferred_element_type=F32)


def dot_lt(a, b):
    return lax.dot_general(a, b, (((0,), (0,)), ((), ())), preferred_element_type=F32)


def row_mean(x):
    return jnp.sum(x, axis=-1, keepdims=True) * (1.0 / D)


def col_sum(x):
    return jnp.sum(x, axis=0, keepdims=True)


def silu_parts(z):
    sig = 0.5 + 0.5 * jnp.tanh(0.5 * z)
    h = z * sig
    return h, sig + h * (1.0 - sig)


def normalize(post):
    centered = post - row_mean(post)
    scale = lax.rsqrt(row_mean(centered * centered) + epsilon)
    return centered * scale, scale


def norm_back(t, normed, scale):
    return scale * (t - row_mean(t) - normed * row_mean(t * normed))


def column_of(row):
    return jnp.transpose(jnp.broadcast_to(row.astype(F32), (LANE, LANE))).astype(I32)


def lanes(base):
    return lax.broadcasted_iota(I32, (LANE, LANE), 1) + base


def hot(mask):
    return jnp.where(mask, 1.0, 0.0).astype(BF16)


class Place:
    def __init__(self):
        self.lat = lax.axis_index("lat")
        self.lon = lax.axis_index("lon")
        self.core = lax.rem(self.lat, 2)
        self.y = lax.div(self.lat, 2)
        self.x = lax.div(self.lon, 4)
        self.z = lax.rem(self.lon, 4)
        self.twin = (self.lat + 1 - 2 * self.core, self.lon)
        self.neighbour = [
            (
                lax.rem(self.lat + (dlat + N_LAT), N_LAT),
                lax.rem(self.lon + (dlon + N_LON), N_LON),
            )
            for dlat, dlon in OFFSETS
        ]
        turn = [[lax.rem(i + d, 4) for d in range(4)] for i in (self.x, self.y, self.z)]
        self.ring = [
            [(self.lat, turn[0][d] * 4 + self.z) for d in range(4)],
            [(turn[1][d] * 2 + self.core, self.lon) for d in range(4)],
            [(self.lat, self.x * 4 + turn[2][d]) for d in range(4)],
        ]
        first, second = 1 - self.core, self.core

        def pick(a, b):
            return first * a + second * b

        self.index = []
        self.peer = []
        for a in range(3):
            b = (a + 1) % 3
            self.index.append([pick(turn[a][d], turn[b][d]) for d in range(4)])
            self.peer.append(
                [
                    tuple(pick(m, n) for m, n in zip(self.ring[a][d], self.ring[b][d]))
                    for d in range(4)
                ]
            )


class Reduce:
    def __init__(self, place, start, gb, rc, s0, r1, s1, r2, s2, r3, fin, send, recv):
        self.p = place
        self.at = [place.index[(start + level) % 3] for level in range(3)]
        self.peer = [place.peer[(start + level) % 3] for level in range(3)]
        self.gb, self.rc, self.s0, self.r1, self.s1 = gb, rc, s0, r1, s1
        self.r2, self.s2, self.r3, self.fin = r2, s2, r3, fin
        self.send, self.recv = send, recv
        self.copies = {}
        self.used = 0

    def pack(self, j, val):
        width = val.shape[1]
        self.gb[:, :, :, j] = val.astype(BF16).reshape(2, 4, 4, 16, width)

    def copy(self, step, src, dst, device):
        c = pltpu.make_async_remote_copy(
            src_ref=src,
            dst_ref=dst,
            send_sem=self.send.at[self.used],
            recv_sem=self.recv.at[self.used],
            device_id=device,
            device_id_type=MESH,
        )
        c.start()
        self.used += 1
        self.copies.setdefault(step, []).append(c)

    def wait(self, step):
        for c in self.copies[step]:
            c.wait_recv()

    def spread(self, step, level, src, dst):
        for d in (2, 1, 3):
            self.copy(step, src(self.at[level][d]), dst(d), self.peer[level][d])

    def step(self, k):
        h = self.p.core
        own, own2 = self.at[0][0], self.at[1][0]
        if k == 0:
            self.copy(0, self.gb.at[1 - h], self.rc, self.p.twin)
        elif k == 1:
            self.wait(0)
            for i in range(4):
                mine = self.gb[h, i].astype(F32)
                self.s0[i] = (mine + self.rc[i].astype(F32)).astype(BF16)
            self.spread(1, 0, lambda i: self.s0.at[i], lambda d: self.r1.at[d - 1])
        elif k == 2:
            self.wait(1)
            total = self.s0[own].astype(F32)
            for d in range(3):
                total += self.r1[d].astype(F32)
            self.s1[...] = total.astype(BF16)
            self.spread(2, 1, lambda i: self.s1.at[i], lambda d: self.r2.at[d - 1])
        elif k == 3:
            self.wait(2)
            total = self.s1[own2].astype(F32)
            for d in range(3):
                total += self.r2[d].astype(F32)
            self.s2[...] = total.astype(BF16)
            self.spread(3, 2, lambda i: self.s2, lambda d: self.r3.at[d - 1])
        elif k == 4:
            self.wait(3)
            near = self.s2[...].astype(F32) + self.r3[1].astype(F32)
            far = self.r3[0].astype(F32) + self.r3[2].astype(F32)
            self.fin[h, own, own2] = (near + far).astype(BF16)
            piece = self.fin.at[h, own, own2]
            self.spread(4, 1, lambda i: piece, lambda d: piece)
        elif k == 5:
            self.wait(4)
            piece = self.fin.at[h, own]
            self.spread(5, 0, lambda i: piece, lambda d: piece)
        elif k == 6:
            self.wait(5)
            self.copy(6, self.fin.at[h], self.fin.at[h], self.p.twin)
        elif k == 7:
            self.wait(6)

    def drain(self):
        for group in self.copies.values():
            for c in group:
                c.wait_send()


class Vectors:
    def __init__(self, place, val, slots, send, recv):
        self.p, self.val, self.slots, self.send, self.recv = place, val, slots, send, recv
        self.copies = []

    def start(self, k):
        axis = k - 1
        hops = [(0, self.p.twin)] if k == 0 else [(d, self.p.ring[axis][d]) for d in (2, 1, 3)]
        for d, device in hops:
            at = 0 if k == 0 else 3 * (k - 1) + d
            c = pltpu.make_async_remote_copy(
                src_ref=self.val.at[k],
                dst_ref=self.slots.at[at],
                send_sem=self.send.at[at],
                recv_sem=self.recv.at[at],
                device_id=device,
                device_id_type=MESH,
            )
            c.start()
            self.copies.append((k, c))

    def finish(self, k):
        for j, c in self.copies:
            if j == k:
                c.wait_recv()
        if k == 0:
            self.val[1] = self.val[0] + self.slots[0]
        else:
            at = 3 * (k - 1)
            near = self.val[k] + self.slots[at + 2]
            far = self.slots[at + 1] + self.slots[at + 3]
            self.val[k + 1] = near + far

    def drain(self):
        for _, c in self.copies:
            c.wait_send()


def layer(
    nodes_h, edges_h, senders, receivers, live, send_rows, cot_h,
    wei_h, eib, weo_h, eob, egain, wni_h, nib, wno_h, nob, ngain,
    new_nodes_h, node_grad_h, edge_grad_h, fin_a_h, fin_b_h, fin_c_h, vec_h,
    nodes, edges, cot, wei, weo, wni, wno,
    ohs, oht, ohr, pre, hid, normed, scale, prnd, staging, post,
    table, grad_rows, zb, halo_out, halo_in, back_out, back_in, sendt,
    new_nodes, node_base, node_grad, summed, sum_acc, outer_acc,
    npre, npost, nhid, npost_round, npre_round, acc,
    bufs_a, bufs_b, bufs_c, vec, vec_slots,
    in_sem, out_sem, halo_send, halo_recv, sems_a, sems_b, sems_c, sems_v,
):
    place = Place()
    prd = ohs

    def load(k, src, dst):
        c = pltpu.make_async_copy(src, dst, in_sem.at[k])
        c.start()
        return c

    def store(k, src, dst):
        c = pltpu.make_async_copy(src, dst, out_sem.at[k])
        c.start()
        return c

    c_nodes = load(0, nodes_h, nodes)
    c_wei = load(1, wei_h, wei)
    c_edges = load(2, edges_h, edges)
    c_wni = load(4, wni_h, wni)
    c_weo = load(3, weo_h, weo)
    c_wno = load(5, wno_h, wno)
    c_cot = load(6, cot_h, cot)

    barrier = pltpu.get_barrier_semaphore()
    partners = place.neighbour + [place.twin]
    for axis in range(3):
        partners += place.ring[axis][1:]
    for device in partners:
        pl.semaphore_signal(barrier, inc=1, device_id=device, device_id_type=MESH)

    red_a = Reduce(place, 0, *bufs_a, *sems_a)
    red_b = Reduce(place, 2, *bufs_b, *sems_b)
    red_c = Reduce(place, 1, *bufs_c, *sems_c)
    red_v = Vectors(place, vec, vec_slots, *sems_v)

    picks = []
    for k in range(2):
        col = column_of(send_rows[:, k * LANE : (k + 1) * LANE])
        picks.append(jnp.concatenate([hot(col == lanes(j * LANE)) for j in range(4)], axis=1))
    picks = jnp.concatenate(picks, axis=0)
    c_nodes.wait()
    halo_out[...] = dot(picks, nodes[...]).astype(BF16).reshape(8, SLOT, D)
    pl.semaphore_wait(barrier, len(partners))

    def exchange(src, dst, base):
        copies = []
        for n in range(8):
            c = pltpu.make_async_remote_copy(
                src_ref=src.at[n],
                dst_ref=dst.at[7 - n],
                send_sem=halo_send.at[base + n],
                recv_sem=halo_recv.at[base + 7 - n],
                device_id=place.neighbour[n],
                device_id_type=MESH,
            )
            c.start()
            copies.append(c)
        return copies

    halo = exchange(halo_out, halo_in, 0)

    rowi = lax.broadcasted_iota(I32, (NODE, LANE), 0)
    for k in range(2):
        row = send_rows[:, k * LANE : (k + 1) * LANE]
        sendt[:, k * LANE : (k + 1) * LANE] = hot(rowi == row)
    acc[...] = jnp.zeros_like(acc)
    c_wei.wait()
    table[0:NODE, :] = dot(nodes[...], wei[D : 2 * D, :]).astype(BF16)
    table[TABLE:WIDE, :] = dot(nodes[...], wei[2 * D : 3 * D, :]).astype(BF16)
    c_edges.wait()

    def early(c, _):
        base = pl.multiple_of(c * CHUNK, CHUNK)
        rows = pl.ds(base, CHUNK)
        pre[rows, :] = dot(edges[rows, :], wei[0:D, :]) + eib[...]
        oht[WIDE:TALL, rows] = jnp.transpose(edges[rows, :])
        for j in range(CHUNK // LANE):
            s_row = senders[pl.ds(c * (CHUNK // LANE) + j, 1), :]
            r_row = receivers[pl.ds(c * (CHUNK // LANE) + j, 1), :]
            s_col, r_col = column_of(s_row), column_of(r_row)
            here = pl.ds(pl.multiple_of(base + j * LANE, LANE), LANE)
            for k in range(TABLE // LANE):
                ohs[here, k * LANE : (k + 1) * LANE] = hot(s_col == lanes(k * LANE))
            for k in range(NODE // LANE):
                ohr[here, k * LANE : (k + 1) * LANE] = hot(r_col == lanes(k * LANE))
            ids = lax.broadcasted_iota(I32, (TABLE, LANE), 0)
            oht[0:TABLE, here] = hot(ids == s_row)
            oht[TABLE:WIDE, here] = hot(rowi == r_row)
        return 0

    lax.fori_loop(0, STEPS, early, 0)
    c_wni.wait()
    npre[...] = dot(nodes[...], wni[0:D, :]) + nib[...]
    c_weo.wait()
    c_wno.wait()
    c_cot.wait()

    for c in halo:
        c.wait_recv()
    table[NODE:TABLE, :] = dot(halo_in[...].reshape(PEER, D), wei[D : 2 * D, :]).astype(BF16)

    def part(t, s):
        return slice(t * PART + s * SUB, t * PART + (s + 1) * SUB)

    def whole(t):
        return slice(t * PART, (t + 1) * PART)

    def live_rows(t, s):
        ids = lax.broadcasted_iota(I32, (SUB, LANE), 0)
        one = jnp.where(ids < live[0] - (t * PART + s * SUB), 1.0, 0.0)
        return jnp.concatenate([one] * (D // LANE), axis=1)

    def fwd_gather(t):
        rows = whole(t)
        z = dot(ohs[rows, :], table[0:TABLE, :]) + dot(ohr[rows, :], table[TABLE:WIDE, :])
        pre[rows, :] += z

    def fwd_silu(t):
        for s in range(SUBS):
            rows = part(t, s)
            h, slope = silu_parts(pre[rows, :])
            hid[rows, :] = h.astype(BF16)
            pre[rows, :] = slope

    def fwd_outer(t):
        post[t % 3] = dot(hid[whole(t), :], weo[...])

    def fwd_norm(t):
        for s in range(SUBS):
            rows = part(t, s)
            unit, inv = normalize(post[t % 3, s * SUB : (s + 1) * SUB, :] + eob[...])
            normed[rows, :] = unit.astype(BF16)
            scale[rows, :] = inv
            new = edges[rows, :].astype(F32) + unit * egain[...]
            prnd[rows, :] = (new * live_rows(t, s)).astype(BF16)

    def fwd_sum(t):
        got = dot(oht[TABLE:WIDE, whole(t)], prnd[whole(t), :])
        if t == 0:
            sum_acc[...] = got
        else:
            sum_acc[...] += got

    def at(f, t):
        if 0 <= t < PARTS:
            f(t)

    for t in range(PARTS + 3):
        at(fwd_gather, t)
        at(fwd_silu, t - 1)
        at(fwd_norm, t - 2)
        at(fwd_outer, t - 1)
        at(fwd_sum, t - 3)
    summed[...] = sum_acc[...].astype(BF16)

    def fold(x):
        return jnp.sum(x.reshape(x.shape[0] // 8, 8, x.shape[1]), axis=0)

    def half(t):
        return slice(t * NPART, (t + 1) * NPART)

    def strip(t, s):
        return slice(t * NPART + s * SUB, t * NPART + (s + 1) * SUB)

    halves = (0, 1)
    for t in halves:
        npre[half(t), :] += dot(summed[half(t), :], wni[D : 2 * D, :])
    for t in halves:
        for s in range(NSUBS):
            rows = strip(t, s)
            h, slope = silu_parts(npre[rows, :])
            nhid[rows, :] = h.astype(BF16)
            npre[rows, :] = slope
        npost[half(t), :] = dot(nhid[half(t), :], wno[...])
    for t in halves:
        for s in range(NSUBS):
            rows = strip(t, s)
            unit, inv = normalize(npost[rows, :] + nob[...])
            new_nodes[rows, :] = (nodes[rows, :].astype(F32) + unit * ngain[...]).astype(BF16)
            cotangent = cot[rows, :].astype(F32)
            acc[5] += fold(cotangent * unit)
            grad = norm_back(cotangent * ngain[...], unit, inv)
            acc[4] += fold(grad)
            npost_round[rows, :] = grad.astype(BF16)
        grad = dot_rt(npost_round[half(t), :], wno[...]) * npre[half(t), :]
        acc[3] += fold(grad)
        npre_round[half(t), :] = grad.astype(BF16)
    for t in halves:
        grad_rows[half(t), :] = dot_rt(npre_round[half(t), :], wni[D : 2 * D, :]).astype(BF16)
    s_nodes = store(0, new_nodes, new_nodes_h)

    def bwd_gather(t):
        post[t % 3] = dot(ohr[whole(t), :], grad_rows[...])

    def bwd_norm(t):
        for s in range(SUBS):
            rows = part(t, s)
            g = post[t % 3, s * SUB : (s + 1) * SUB, :] * live_rows(t, s)
            unit = normed[rows, :].astype(F32)
            acc[2] += fold(g * unit)
            grad = norm_back(g * egain[...], unit, scale[rows, :])
            acc[1] += fold(grad)
            prnd[rows, :] = grad.astype(BF16)

    def bwd_outer(t):
        got = dot_lt(hid[whole(t), :], prnd[whole(t), :])
        if t == 0:
            outer_acc[...] = got
        else:
            outer_acc[...] += got

    for t in range(PARTS + 2):
        at(bwd_gather, t)
        if t == 0:
            node_outer = dot_lt(nhid[...], npost_round[...])
            red_a.pack(2, node_outer)
            red_a.pack(0, dot_lt(nodes[...], npre_round[...]))
            red_a.pack(1, dot_lt(summed[...], npre_round[...]))
        at(bwd_norm, t - 1)
        if t == 1:
            red_a.step(0)
        if t == 2:
            node_base[...] = cot[...].astype(F32) + dot_rt(npre_round[...], wni[0:D, :])
        at(bwd_outer, t - 2)
    left, right = slice(0, D // 2), slice(D // 2, D)
    red_b.pack(3, outer_acc[:, left])
    red_b.pack(4, outer_acc[:, right])
    red_a.step(1)

    def bwd_inner(t, cols):
        grad = dot_rt(prnd[whole(t), :], weo[cols, :]) * pre[whole(t), cols]
        acc[0, :, cols] += fold(grad)
        prd[whole(t), cols] = grad.astype(BF16)

    def tall(red, cols):
        got = dot(oht[...], prd[:, cols])
        zb[:, cols] = got[0:WIDE].astype(BF16)
        red.pack(0, got[WIDE:TALL])

    def inner_sums(red, cols):
        incoming = halo_in[...].reshape(PEER, D)
        red.pack(1, dot_lt(nodes[...], zb[0:NODE, cols]) + dot_lt(incoming, zb[NODE:TABLE, cols]))
        red.pack(2, dot_lt(nodes[...], zb[TABLE:WIDE, cols]))
        red.step(0)

    for t in range(PARTS):
        bwd_inner(t, left)
    tall(red_b, left)
    for t in range(PARTS):
        bwd_inner(t, right)
    inner_sums(red_b, left)
    red_a.step(2)
    vec[0, 0:6, :] = jnp.sum(acc[...], axis=1)
    vec[0, 6:8, :] = jnp.zeros((2, D), F32)
    red_v.start(0)
    tall(red_c, right)
    red_b.step(1)
    inner_sums(red_c, right)
    red_a.step(3)
    red_v.finish(0)
    red_v.start(1)

    back = dot_rt(zb[NODE:TABLE, :], wei[D : 2 * D, :]).astype(BF16)
    back_out[...] = back.reshape(8, SLOT, D)
    returning = exchange(back_out, back_in, 8)
    red_c.step(1)
    red_a.step(4)
    stores = []

    def edge_out(c):
        rows = pl.ds(c * CHUNK, CHUNK)
        grad = dot_rt(prd[rows, 0:D], wei[0:D, :]) + dot(ohr[rows, :], grad_rows[...])
        alive = lax.broadcasted_iota(I32, (CHUNK, D), 0) < live[0] - c * CHUNK
        staging[rows, :] = jnp.where(alive, grad, 0.0).astype(BF16)
        stores.append(store(2 + c, staging.at[rows], edge_grad_h.at[rows]))

    edge_out(0)
    red_b.step(2)
    red_c.step(2)
    red_v.finish(1)
    red_v.start(2)
    red_a.step(5)
    edge_out(1)
    red_b.step(3)
    red_c.step(3)
    edge_out(2)
    red_b.step(4)
    red_c.step(4)
    red_v.finish(2)
    red_v.start(3)
    red_a.step(6)
    edge_out(3)
    red_b.step(5)
    red_c.step(5)
    node_base[...] += dot_rt(zb[0:NODE, :], wei[D : 2 * D, :])
    node_base[...] += dot_rt(zb[TABLE:WIDE, :], wei[2 * D : 3 * D, :])
    for c in returning:
        c.wait_recv()
    owned = dot(sendt[...], back_in[...].reshape(PEER, D))
    node_grad[...] = (node_base[...] + owned).astype(BF16)
    stores.append(store(1, node_grad, node_grad_h))
    red_v.finish(3)
    stores.append(store(6, vec.at[4], vec_h))
    red_a.step(7)
    stores.append(store(7, red_a.fin, fin_a_h))
    red_b.step(6)
    red_c.step(6)
    red_b.step(7)
    stores.append(store(8, red_b.fin, fin_b_h))
    red_c.step(7)
    stores.append(store(9, red_c.fin, fin_c_h))
    for c in halo + returning:
        c.wait_send()
    for red in (red_a, red_b, red_c, red_v):
        red.drain()
    s_nodes.wait()
    for c in stores:
        c.wait()


def fin_shape(nb, width):
    return (2, 4, 4, nb, 16, width)


FINS = ((3, D), (5, D // 2), (3, D // 2))


def reduce_bufs(nb, width):
    tile = (nb, 16, width)
    return (
        pltpu.VMEM(fin_shape(nb, width), BF16),
        pltpu.VMEM((4, 4) + tile, BF16),
        pltpu.VMEM((4, 4) + tile, BF16),
        pltpu.VMEM((3, 4) + tile, BF16),
        pltpu.VMEM((4,) + tile, BF16),
        pltpu.VMEM((3,) + tile, BF16),
        pltpu.VMEM(tile, BF16),
        pltpu.VMEM((3,) + tile, BF16),
        pltpu.VMEM(fin_shape(nb, width), BF16),
    )


def sem_pair(n):
    return (pltpu.SemaphoreType.DMA((n,)), pltpu.SemaphoreType.DMA((n,)))


def widen(
    fa, fb, fc, vec, new_nodes, node_grad, edge_grad,
    new_nodes_o, node_grad_o, edge_grad_o, edge_inner, edge_outer, node_inner, node_outer,
    v0, v1, v2, v3, v4, v5,
    va, vb, vc, vn, vg, ve, wide, in_sem, out_sem,
):
    outs = []

    def load(k, src, dst):
        c = pltpu.make_async_copy(src, dst, in_sem.at[k])
        c.start()
        return c

    def store(k, src, dst):
        c = pltpu.make_async_copy(src, dst, out_sem.at[k])
        c.start()
        outs.append(c)

    c_a = [load(h, fa.at[h], va.at[h]) for h in range(2)]
    c_b = [load(2 + h, fb.at[h], vb.at[h]) for h in range(2)]
    c_c = [load(4 + h, fc.at[h], vc.at[h]) for h in range(2)]
    c_e = [load(7 + k, edge_grad.at[pl.ds(k * 512, 512)], ve.at[pl.ds(k * 512, 512)]) for k in range(4)]
    c_n = load(11, new_nodes, vn)
    c_g = load(12, node_grad, vg)
    k_out = 0
    HALF = NODE // 2

    places = ((node_inner, 0), (node_inner, 512), (node_outer, 0))
    for h in range(2):
        c_a[h].wait()
        for j, (out, first) in enumerate(places):
            rows = pl.ds(j * 512 + h * HALF, HALF)
            wide[rows, :] = va[h, :, :, j].reshape(HALF, D).astype(F32)
            store(k_out, wide.at[rows], out.at[pl.ds(first + h * HALF, HALF)])
            k_out += 1
    for h in range(2):
        c_b[h].wait()
        c_c[h].wait()
        for j in range(3):
            rows = pl.ds(1536 + j * 512 + h * HALF, HALF)
            wide[rows, 0:HALF] = vb[h, :, :, j].reshape(HALF, HALF).astype(F32)
            wide[rows, HALF:D] = vc[h, :, :, j].reshape(HALF, HALF).astype(F32)
            store(k_out, wide.at[rows], edge_inner.at[pl.ds(j * 512 + h * HALF, HALF)])
            k_out += 1
    for h in range(2):
        rows = pl.ds(3072 + h * HALF, HALF)
        for j in range(2):
            wide[rows, j * HALF : (j + 1) * HALF] = vb[h, :, :, 3 + j].reshape(HALF, HALF).astype(F32)
        store(k_out, wide.at[rows], edge_outer.at[pl.ds(h * HALF, HALF)])
        k_out += 1
    for k in range(4):
        c_e[k].wait()
        store(k_out, ve.at[pl.ds(k * 512, 512)], edge_grad_o.at[pl.ds(k * 512, 512)])
        k_out += 1
    c_n.wait()
    store(k_out, vn, new_nodes_o)
    c_g.wait()
    store(k_out + 1, vg, node_grad_o)
    for k, out in enumerate((v0, v1, v2, v3, v4, v5)):
        out[...] = vec[k : k + 1, :]
    for c in outs:
        c.wait()


def unpack(outs):
    new_nodes, node_grad, edge_grad, fa, fb, fc, vec = outs
    hbm = pl.BlockSpec(memory_space=pl.ANY)
    vm = pl.BlockSpec(memory_space=pltpu.VMEM)
    shapes = [
        ((NODE, D), BF16), ((NODE, D), BF16), ((EDGE, D), BF16),
        ((3 * D, D), F32), ((D, D), F32), ((2 * D, D), F32), ((D, D), F32),
    ] + [((1, D), F32)] * 6
    scratch = [pltpu.VMEM(fin_shape(*f), BF16) for f in FINS]
    return pl.pallas_call(
        widen,
        out_shape=[jax.ShapeDtypeStruct(s, t) for s, t in shapes],
        in_specs=[hbm] * 3 + [vm] + [hbm] * 3,
        out_specs=[hbm] * 7 + [vm] * 6,
        scratch_shapes=scratch + [
            pltpu.VMEM((NODE, D), BF16), pltpu.VMEM((NODE, D), BF16), pltpu.VMEM((EDGE, D), BF16),
            pltpu.VMEM((7 * D, D), F32),
            pltpu.SemaphoreType.DMA((13,)), pltpu.SemaphoreType.DMA((20,)),
        ],
        compiler_params=pltpu.CompilerParams(vmem_limit_bytes=63 * 2**20),
        name="widen",
    )(fa, fb, fc, vec, new_nodes, node_grad, edge_grad)


def body(
    node_states, edge_states, senders, receivers, live_count, send_rows, node_cotangent,
    edge_inner, edge_inbias, edge_outer, edge_outbias, edge_gain,
    node_inner, node_inbias, node_outer, node_outbias, node_gain,
):
    hbm = pl.BlockSpec(memory_space=pl.ANY)
    vm = pl.BlockSpec(memory_space=pltpu.VMEM)
    sm = pl.BlockSpec(memory_space=pltpu.SMEM)

    def row(v):
        return v.reshape(1, D)

    def v(shape, dtype=BF16):
        return pltpu.VMEM(shape, dtype)

    outs = pl.pallas_call(
        layer,
        out_shape=[
            jax.ShapeDtypeStruct((NODE, D), BF16),
            jax.ShapeDtypeStruct((NODE, D), BF16),
            jax.ShapeDtypeStruct((EDGE, D), BF16),
        ]
        + [jax.ShapeDtypeStruct(fin_shape(*f), BF16) for f in FINS]
        + [jax.ShapeDtypeStruct((8, D), F32)],
        in_specs=[
            hbm, hbm, vm, vm, sm, vm, hbm,
            hbm, vm, hbm, vm, vm, hbm, vm, hbm, vm, vm,
        ],
        out_specs=[hbm] * 7,
        scratch_shapes=[
            v((NODE, D)), v((EDGE, D)), v((NODE, D)),
            v((3 * D, D)), v((D, D)), v((2 * D, D)), v((D, D)),
            v((EDGE, TABLE)), v((TALL, EDGE)), v((EDGE, NODE)),
            v((EDGE, D), F32), v((EDGE, D)), v((EDGE, D)), v((EDGE, 1), F32),
            v((EDGE, D)), v((EDGE, D)), v((3, PART, D), F32),
            v((WIDE, D)), v((NODE, D)), v((WIDE, D)),
            v((8, SLOT, D)), v((8, SLOT, D)), v((8, SLOT, D)), v((8, SLOT, D)),
            v((NODE, PEER)),
            v((NODE, D)), v((NODE, D), F32), v((NODE, D)), v((NODE, D)),
            v((NODE, D), F32), v((D, D), F32),
            v((NODE, D), F32), v((NODE, D), F32), v((NODE, D)), v((NODE, D)), v((NODE, D)),
            v((6, 8, D), F32),
        ]
        + [reduce_bufs(*f) for f in FINS]
        + [
            v((5, 8, D), F32), v((10, 8, D), F32),
            pltpu.SemaphoreType.DMA((7,)), pltpu.SemaphoreType.DMA((11,)),
            pltpu.SemaphoreType.DMA((16,)), pltpu.SemaphoreType.DMA((16,)),
            sem_pair(17), sem_pair(17), sem_pair(17), sem_pair(10),
        ],
        compiler_params=pltpu.CompilerParams(
            collective_id=0, has_side_effects=True, vmem_limit_bytes=63 * 2**20
        ),
        name="layer",
    )(
        node_states, edge_states, senders.reshape(16, LANE), receivers.reshape(16, LANE),
        live_count, send_rows, node_cotangent,
        edge_inner, row(edge_inbias), edge_outer, row(edge_outbias), row(edge_gain),
        node_inner, row(node_inbias), node_outer, row(node_outbias), row(node_gain),
    )
    new_nodes, node_grad, edge_grad, ei, eo, ni, no, *vecs = unpack(outs)
    vecs = [x.reshape(D) for x in vecs]
    return (
        new_nodes, node_grad, edge_grad,
        ei, vecs[0], eo, vecs[1], vecs[2],
        ni, vecs[3], no, vecs[4], vecs[5],
    )


def solution(mesh):
    nodes = P(("lat", "lon"), None)
    flat = P(("lat", "lon"))
    return jax.shard_map(
        body,
        mesh=mesh,
        in_specs=(nodes, nodes, flat, flat, flat, nodes, nodes) + (P(),) * 10,
        out_specs=(nodes, nodes, nodes) + (P(),) * 10,
        check_vma=False,
    )
```

```python
import functools

import jax
import jax.numpy as jnp
from jax import lax
from jax.experimental import pallas as pl
from jax.experimental.pallas import tpu as pltpu
from jax.sharding import PartitionSpec as P

MESH = pl.DeviceIdType.MESH
F32 = jnp.float32
BF16 = jnp.bfloat16
I32 = jnp.int32
epsilon = 1e-05

D = 512
NODE = 512
EDGE = 2048
SLOT = 32
PEER = 256
TABLE = NODE + PEER
WIDE = TABLE + NODE
CHUNK = 512
STEPS = EDGE // CHUNK
PART = 512
NPART = 256
NSUBS = NPART // 32
TALL = NODE + PEER + NODE + D
PARTS = EDGE // PART
SUB = 32
SUBS = PART // SUB
LANE = 128
N_LAT = 8
N_LON = 16
OFFSETS = ((-1, -1), (-1, 0), (-1, 1), (0, -1), (0, 1), (1, -1), (1, 0), (1, 1))


def dot(a, b):
    return jnp.dot(a, b, preferred_element_type=F32)


def dot_rt(a, b):
    return lax.dot_general(a, b, (((1,), (1,)), ((), ())), preferred_element_type=F32)


def dot_lt(a, b):
    return lax.dot_general(a, b, (((0,), (0,)), ((), ())), preferred_element_type=F32)


def row_mean(x):
    return jnp.sum(x, axis=-1, keepdims=True) * (1.0 / D)


def col_sum(x):
    return jnp.sum(x, axis=0, keepdims=True)


def silu_parts(z):
    sig = 0.5 + 0.5 * jnp.tanh(0.5 * z)
    h = z * sig
    return h, sig + h * (1.0 - sig)


def normalize(post):
    centered = post - row_mean(post)
    scale = lax.rsqrt(row_mean(centered * centered) + epsilon)
    return centered * scale, scale


def norm_back(t, normed, scale):
    return scale * (t - row_mean(t) - normed * row_mean(t * normed))


def column_of(row):
    return jnp.transpose(jnp.broadcast_to(row.astype(F32), (LANE, LANE))).astype(I32)


def lanes(base):
    return lax.broadcasted_iota(I32, (LANE, LANE), 1) + base


def hot(mask):
    return jnp.where(mask, 1.0, 0.0).astype(BF16)


class Place:
    def __init__(self):
        lat = lax.axis_index("lat")
        lon = lax.axis_index("lon")
        self.core = lax.rem(lat, 2)
        at = (lax.div(lon, 4), lax.div(lat, 2), lax.rem(lon, 4))
        self.twin = (lat + 1 - 2 * self.core, lon)
        self.neighbour = [
            (lax.rem(lat + (dlat + N_LAT), N_LAT), lax.rem(lon + (dlon + N_LON), N_LON))
            for dlat, dlon in OFFSETS
        ]
        one, two = 1 - self.core, self.core
        self.bit, mate = {}, {}
        for a, i in enumerate(at):
            low, upper = lax.rem(i, 2), lax.div(i, 2)
            odd = low + upper - 2 * low * upper
            near, far = i + 1 - 2 * low, 3 - i
            self.bit[a, 0] = one * odd + two * upper
            self.bit[a, 1] = one * upper + two * odd
            mate[a, 0] = one * near + two * far
            mate[a, 1] = one * far + two * near
        known = {}

        def device(flips):
            if flips not in known:
                x, y, z = [
                    mate[a, 0] if (a, 0) in flips else mate[a, 1] if (a, 1) in flips else at[a]
                    for a in range(3)
                ]
                known[flips] = (y * 2 + self.core, x * 4 + z)
            return known[flips]

        self.level = []
        for n in range(3):
            a, b, c = n, (n + 1) % 3, (n + 2) % 3
            squares = (((a, 0), (b, 0)), ((c, 0), (a, 1)), ((b, 1), (c, 1)))
            self.level.append([])
            for p, q in squares:
                bp, bq = self.bit[p], self.bit[q]
                partners = {
                    1: (2 * bp + 1 - bq, device(frozenset((q,)))),
                    2: (2 - 2 * bp + bq, device(frozenset((p,)))),
                    3: (2 - 2 * bp + 1 - bq, device(frozenset((p, q)))),
                }
                self.level[n].append((2 * bp + bq, partners))
        self.partners = self.neighbour + [self.twin] + list(known.values())


class Reduce:
    def __init__(self, place, streams, gb, rc, s0, r1, s1, r2, s2, r3, fin, send, recv):
        self.p, self.streams = place, streams
        self.gb, self.rc, self.s0, self.r1, self.s1 = gb, rc, s0, r1, s1
        self.r2, self.s2, self.r3, self.fin = r2, s2, r3, fin
        self.send, self.recv = send, recv
        self.copies = {}
        self.used = 0

    def pack(self, j, val):
        width = val.shape[1]
        self.gb[:, j] = val.astype(BF16).reshape(2, 4, 4, 16, width)

    def copy(self, step, src, dst, device):
        c = pltpu.make_async_remote_copy(
            src_ref=src,
            dst_ref=dst,
            send_sem=self.send.at[self.used],
            recv_sem=self.recv.at[self.used],
            device_id=device,
            device_id_type=MESH,
        )
        c.start()
        self.used += 1
        self.copies.setdefault(step, []).append(c)

    def wait(self, step):
        for c in self.copies[step]:
            c.wait_recv()

    def spread(self, step, level, src, dst):
        for d in (3, 1, 2):
            for n, part in enumerate(self.streams):
                there, device = self.p.level[n][level][1][d]
                self.copy(step, src(n, part, there), dst(n, part, d), device)

    def step(self, k):
        h = self.p.core
        own = [self.p.level[n][0][0] for n in range(3)]
        own2 = [self.p.level[n][1][0] for n in range(3)]
        blocks = self.gb.shape[1]
        if k == 0:
            for j in range(blocks):
                self.copy(0, self.gb.at[1 - h, j], self.rc.at[j], self.p.twin)
        elif k == 1:
            self.wait(0)
            for part in self.streams:
                mine = self.gb[h, part].astype(F32)
                self.s0[part] = (mine + self.rc[part].astype(F32)).astype(BF16)
            self.spread(
                1, 0, lambda n, part, i: self.s0.at[part, i], lambda n, part, d: self.r1.at[d - 1, part]
            )
        elif k == 2:
            self.wait(1)
            for n, part in enumerate(self.streams):
                total = self.s0[part, own[n]].astype(F32)
                for d in range(3):
                    total += self.r1[d, part].astype(F32)
                self.s1[part] = total.astype(BF16)
            self.spread(
                2, 1, lambda n, part, i: self.s1.at[part, i], lambda n, part, d: self.r2.at[d - 1, part]
            )
        elif k == 3:
            self.wait(2)
            for n, part in enumerate(self.streams):
                total = self.s1[part, own2[n]].astype(F32)
                for d in range(3):
                    total += self.r2[d, part].astype(F32)
                self.s2[part] = total.astype(BF16)
            self.spread(
                3, 2, lambda n, part, i: self.s2.at[part], lambda n, part, d: self.r3.at[d - 1, part]
            )
        elif k == 4:
            self.wait(3)
            for n, part in enumerate(self.streams):
                near = self.s2[part].astype(F32) + self.r3[0, part].astype(F32)
                far = self.r3[1, part].astype(F32) + self.r3[2, part].astype(F32)
                self.fin[h, part, own[n], own2[n]] = (near + far).astype(BF16)

            def piece(n, part, _):
                return self.fin.at[h, part, own[n], own2[n]]

            self.spread(4, 1, piece, piece)
        elif k == 5:
            self.wait(4)

            def piece(n, part, _):
                return self.fin.at[h, part, own[n]]

            self.spread(5, 0, piece, piece)
        elif k == 6:
            self.wait(5)
            for j in range(blocks):
                self.copy(6, self.fin.at[h, j], self.fin.at[h, j], self.p.twin)
        elif k == 7:
            self.wait(6)

    def drain(self):
        for group in self.copies.values():
            for c in group:
                c.wait_send()


class Vectors:
    def __init__(self, place, val, slots, send, recv):
        self.p, self.val, self.slots, self.send, self.recv = place, val, slots, send, recv
        self.copies = []

    def start(self, k):
        hops = [(0, self.p.twin)]
        if k:
            hops = [(d, self.p.level[0][k - 1][1][d][1]) for d in (3, 1, 2)]
        for d, device in hops:
            at = 0 if k == 0 else 3 * (k - 1) + d
            c = pltpu.make_async_remote_copy(
                src_ref=self.val.at[k],
                dst_ref=self.slots.at[at],
                send_sem=self.send.at[at],
                recv_sem=self.recv.at[at],
                device_id=device,
                device_id_type=MESH,
            )
            c.start()
            self.copies.append((k, c))

    def finish(self, k):
        for j, c in self.copies:
            if j == k:
                c.wait_recv()
        if k == 0:
            self.val[1] = self.val[0] + self.slots[0]
        else:
            at = 3 * (k - 1)
            near = self.val[k] + self.slots[at + 1]
            far = self.slots[at + 2] + self.slots[at + 3]
            self.val[k + 1] = near + far

    def drain(self):
        for _, c in self.copies:
            c.wait_send()


def layer(
    nodes_h, edges_h, senders, receivers, live, send_rows, cot_h,
    wei_h, eib, weo_h, eob, egain, wni_h, nib, wno_h, nob, ngain,
    new_nodes_h, node_grad_h, edge_grad_h, fin_a_h, fin_b_h, fin_c_h, vec_h,
    nodes, edges, cot, wei, weo, wni, wno,
    ohs, oht, ohr, pre, hid, normed, scale, prnd, staging, post,
    table, grad_rows, zb, halo_out, halo_in, back_out, back_in, sendt,
    new_nodes, node_base, node_grad, summed, sum_acc, outer_acc,
    npre, npost, nhid, npost_round, npre_round, acc,
    bufs_a, bufs_b, bufs_c, vec, vec_slots,
    in_sem, out_sem, halo_send, halo_recv, sems_a, sems_b, sems_c, sems_v,
):
    place = Place()
    prd = ohs

    def load(k, src, dst):
        c = pltpu.make_async_copy(src, dst, in_sem.at[k])
        c.start()
        return c

    def store(k, src, dst):
        c = pltpu.make_async_copy(src, dst, out_sem.at[k])
        c.start()
        return c

    c_nodes = load(0, nodes_h, nodes)
    c_wei = load(1, wei_h, wei)
    c_edges = load(2, edges_h, edges)
    c_wni = load(4, wni_h, wni)
    c_weo = load(3, weo_h, weo)
    c_wno = load(5, wno_h, wno)
    c_cot = load(6, cot_h, cot)

    barrier = pltpu.get_barrier_semaphore()
    partners = place.partners
    for device in partners:
        pl.semaphore_signal(barrier, inc=1, device_id=device, device_id_type=MESH)

    thirds = (slice(0, 1), slice(1, 2), slice(2, 3))
    red_a = Reduce(place, thirds, *bufs_a, *sems_a)
    red_b = Reduce(place, (slice(0, 2), slice(2, 4), slice(4, 5)), *bufs_b, *sems_b)
    red_c = Reduce(place, thirds, *bufs_c, *sems_c)
    red_v = Vectors(place, vec, vec_slots, *sems_v)

    picks = []
    for k in range(2):
        col = column_of(send_rows[:, k * LANE : (k + 1) * LANE])
        picks.append(jnp.concatenate([hot(col == lanes(j * LANE)) for j in range(4)], axis=1))
    picks = jnp.concatenate(picks, axis=0)
    c_nodes.wait()
    halo_out[...] = dot(picks, nodes[...]).astype(BF16).reshape(8, SLOT, D)
    pl.semaphore_wait(barrier, len(partners))

    def exchange(src, dst, base):
        copies = []
        for n in range(8):
            c = pltpu.make_async_remote_copy(
                src_ref=src.at[n],
                dst_ref=dst.at[7 - n],
                send_sem=halo_send.at[base + n],
                recv_sem=halo_recv.at[base + 7 - n],
                device_id=place.neighbour[n],
                device_id_type=MESH,
            )
            c.start()
            copies.append(c)
        return copies

    halo = exchange(halo_out, halo_in, 0)

    rowi = lax.broadcasted_iota(I32, (NODE, LANE), 0)
    for k in range(2):
        row = send_rows[:, k * LANE : (k + 1) * LANE]
        sendt[:, k * LANE : (k + 1) * LANE] = hot(rowi == row)
    acc[...] = jnp.zeros_like(acc)
    c_wei.wait()
    table[0:NODE, :] = dot(nodes[...], wei[D : 2 * D, :]).astype(BF16)
    table[TABLE:WIDE, :] = dot(nodes[...], wei[2 * D : 3 * D, :]).astype(BF16)
    c_edges.wait()

    def early(c, _):
        base = pl.multiple_of(c * CHUNK, CHUNK)
        rows = pl.ds(base, CHUNK)
        pre[rows, :] = dot(edges[rows, :], wei[0:D, :]) + eib[...]
        oht[WIDE:TALL, rows] = jnp.transpose(edges[rows, :])
        for j in range(CHUNK // LANE):
            s_row = senders[pl.ds(c * (CHUNK // LANE) + j, 1), :]
            r_row = receivers[pl.ds(c * (CHUNK // LANE) + j, 1), :]
            s_col, r_col = column_of(s_row), column_of(r_row)
            here = pl.ds(pl.multiple_of(base + j * LANE, LANE), LANE)
            for k in range(TABLE // LANE):
                ohs[here, k * LANE : (k + 1) * LANE] = hot(s_col == lanes(k * LANE))
            for k in range(NODE // LANE):
                ohr[here, k * LANE : (k + 1) * LANE] = hot(r_col == lanes(k * LANE))
            ids = lax.broadcasted_iota(I32, (TABLE, LANE), 0)
            oht[0:TABLE, here] = hot(ids == s_row)
            oht[TABLE:WIDE, here] = hot(rowi == r_row)
        return 0

    lax.fori_loop(0, STEPS, early, 0)
    c_wni.wait()
    npre[...] = dot(nodes[...], wni[0:D, :]) + nib[...]
    c_weo.wait()
    c_wno.wait()
    c_cot.wait()

    for c in halo:
        c.wait_recv()
    table[NODE:TABLE, :] = dot(halo_in[...].reshape(PEER, D), wei[D : 2 * D, :]).astype(BF16)

    def part(t, s):
        return slice(t * PART + s * SUB, t * PART + (s + 1) * SUB)

    def whole(t):
        return slice(t * PART, (t + 1) * PART)

    def live_rows(t, s):
        ids = lax.broadcasted_iota(I32, (SUB, LANE), 0)
        one = jnp.where(ids < live[0] - (t * PART + s * SUB), 1.0, 0.0)
        return jnp.concatenate([one] * (D // LANE), axis=1)

    def fwd_gather(t):
        rows = whole(t)
        z = dot(ohs[rows, :], table[0:TABLE, :]) + dot(ohr[rows, :], table[TABLE:WIDE, :])
        pre[rows, :] += z

    def fwd_silu(t):
        for s in range(SUBS):
            rows = part(t, s)
            h, slope = silu_parts(pre[rows, :])
            hid[rows, :] = h.astype(BF16)
            pre[rows, :] = slope

    def fwd_outer(t):
        post[t % 3] = dot(hid[whole(t), :], weo[...])

    def fwd_norm(t):
        for s in range(SUBS):
            rows = part(t, s)
            unit, inv = normalize(post[t % 3, s * SUB : (s + 1) * SUB, :] + eob[...])
            normed[rows, :] = unit.astype(BF16)
            scale[rows, :] = inv
            new = edges[rows, :].astype(F32) + unit * egain[...]
            prnd[rows, :] = (new * live_rows(t, s)).astype(BF16)

    def fwd_sum(t):
        got = dot(oht[TABLE:WIDE, whole(t)], prnd[whole(t), :])
        if t == 0:
            sum_acc[...] = got
        else:
            sum_acc[...] += got

    def at(f, t):
        if 0 <= t < PARTS:
            f(t)

    for t in range(PARTS + 3):
        at(fwd_gather, t)
        at(fwd_silu, t - 1)
        at(fwd_norm, t - 2)
        at(fwd_outer, t - 1)
        at(fwd_sum, t - 3)
    summed[...] = sum_acc[...].astype(BF16)

    def fold(x):
        return jnp.sum(x.reshape(x.shape[0] // 8, 8, x.shape[1]), axis=0)

    def half(t):
        return slice(t * NPART, (t + 1) * NPART)

    def strip(t, s):
        return slice(t * NPART + s * SUB, t * NPART + (s + 1) * SUB)

    halves = (0, 1)
    for t in halves:
        npre[half(t), :] += dot(summed[half(t), :], wni[D : 2 * D, :])
    for t in halves:
        for s in range(NSUBS):
            rows = strip(t, s)
            h, slope = silu_parts(npre[rows, :])
            nhid[rows, :] = h.astype(BF16)
            npre[rows, :] = slope
        npost[half(t), :] = dot(nhid[half(t), :], wno[...])
    for t in halves:
        for s in range(NSUBS):
            rows = strip(t, s)
            unit, inv = normalize(npost[rows, :] + nob[...])
            new_nodes[rows, :] = (nodes[rows, :].astype(F32) + unit * ngain[...]).astype(BF16)
            cotangent = cot[rows, :].astype(F32)
            acc[5] += fold(cotangent * unit)
            grad = norm_back(cotangent * ngain[...], unit, inv)
            acc[4] += fold(grad)
            npost_round[rows, :] = grad.astype(BF16)
        grad = dot_rt(npost_round[half(t), :], wno[...]) * npre[half(t), :]
        acc[3] += fold(grad)
        npre_round[half(t), :] = grad.astype(BF16)
    for t in halves:
        grad_rows[half(t), :] = dot_rt(npre_round[half(t), :], wni[D : 2 * D, :]).astype(BF16)
    s_nodes = store(0, new_nodes, new_nodes_h)

    def bwd_gather(t):
        post[t % 3] = dot(ohr[whole(t), :], grad_rows[...])

    def bwd_norm(t):
        for s in range(SUBS):
            rows = part(t, s)
            g = post[t % 3, s * SUB : (s + 1) * SUB, :] * live_rows(t, s)
            unit = normed[rows, :].astype(F32)
            acc[2] += fold(g * unit)
            grad = norm_back(g * egain[...], unit, scale[rows, :])
            acc[1] += fold(grad)
            prnd[rows, :] = grad.astype(BF16)

    def bwd_outer(t):
        got = dot_lt(hid[whole(t), :], prnd[whole(t), :])
        if t == 0:
            outer_acc[...] = got
        else:
            outer_acc[...] += got

    for t in range(PARTS + 2):
        at(bwd_gather, t)
        if t == 0:
            node_outer = dot_lt(nhid[...], npost_round[...])
            red_a.pack(2, node_outer)
            red_a.pack(0, dot_lt(nodes[...], npre_round[...]))
            red_a.pack(1, dot_lt(summed[...], npre_round[...]))
        at(bwd_norm, t - 1)
        if t == 1:
            red_a.step(0)
        if t == 2:
            node_base[...] = cot[...].astype(F32) + dot_rt(npre_round[...], wni[0:D, :])
        at(bwd_outer, t - 2)
    left, right = slice(0, D // 2), slice(D // 2, D)
    red_b.pack(3, outer_acc[:, left])
    red_b.pack(4, outer_acc[:, right])
    red_a.step(1)

    def bwd_inner(t, cols):
        grad = dot_rt(prnd[whole(t), :], weo[cols, :]) * pre[whole(t), cols]
        acc[0, :, cols] += fold(grad)
        prd[whole(t), cols] = grad.astype(BF16)

    def tall(red, cols):
        got = dot(oht[...], prd[:, cols])
        zb[:, cols] = got[0:WIDE].astype(BF16)
        red.pack(0, got[WIDE:TALL])

    def inner_sums(red, cols):
        incoming = halo_in[...].reshape(PEER, D)
        red.pack(1, dot_lt(nodes[...], zb[0:NODE, cols]) + dot_lt(incoming, zb[NODE:TABLE, cols]))
        red.pack(2, dot_lt(nodes[...], zb[TABLE:WIDE, cols]))
        red.step(0)

    for t in range(PARTS):
        bwd_inner(t, left)
    tall(red_b, left)
    for t in range(PARTS):
        bwd_inner(t, right)
    inner_sums(red_b, left)
    red_a.step(2)
    vec[0, 0:6, :] = jnp.sum(acc[...], axis=1)
    vec[0, 6:8, :] = jnp.zeros((2, D), F32)
    red_v.start(0)
    tall(red_c, right)
    red_b.step(1)
    inner_sums(red_c, right)
    red_a.step(3)
    red_v.finish(0)
    red_v.start(1)

    back = dot_rt(zb[NODE:TABLE, :], wei[D : 2 * D, :]).astype(BF16)
    back_out[...] = back.reshape(8, SLOT, D)
    returning = exchange(back_out, back_in, 8)
    red_c.step(1)
    red_a.step(4)
    stores = []

    def edge_out(c):
        rows = pl.ds(c * CHUNK, CHUNK)
        grad = dot_rt(prd[rows, 0:D], wei[0:D, :]) + dot(ohr[rows, :], grad_rows[...])
        alive = lax.broadcasted_iota(I32, (CHUNK, D), 0) < live[0] - c * CHUNK
        staging[rows, :] = jnp.where(alive, grad, 0.0).astype(BF16)
        stores.append(store(2 + c, staging.at[rows], edge_grad_h.at[rows]))

    edge_out(0)
    red_b.step(2)
    red_c.step(2)
    red_v.finish(1)
    red_v.start(2)
    red_a.step(5)
    edge_out(1)
    red_b.step(3)
    red_c.step(3)
    edge_out(2)
    red_b.step(4)
    red_c.step(4)
    red_v.finish(2)
    red_v.start(3)
    red_a.step(6)
    edge_out(3)
    red_b.step(5)
    red_c.step(5)
    node_base[...] += dot_rt(zb[0:NODE, :], wei[D : 2 * D, :])
    node_base[...] += dot_rt(zb[TABLE:WIDE, :], wei[2 * D : 3 * D, :])
    for c in returning:
        c.wait_recv()
    owned = dot(sendt[...], back_in[...].reshape(PEER, D))
    node_grad[...] = (node_base[...] + owned).astype(BF16)
    stores.append(store(1, node_grad, node_grad_h))
    red_v.finish(3)
    stores.append(store(6, vec.at[4], vec_h))
    red_a.step(7)
    stores.append(store(7, red_a.fin, fin_a_h))
    red_b.step(6)
    red_c.step(6)
    red_b.step(7)
    stores.append(store(8, red_b.fin, fin_b_h))
    red_c.step(7)
    stores.append(store(9, red_c.fin, fin_c_h))
    for c in halo + returning:
        c.wait_send()
    for red in (red_a, red_b, red_c, red_v):
        red.drain()
    s_nodes.wait()
    for c in stores:
        c.wait()


def fin_shape(nb, width):
    return (2, nb, 4, 4, 16, width)


FINS = ((3, D), (5, D // 2), (3, D // 2))


def reduce_bufs(nb, width):
    tile = (16, width)
    return (
        pltpu.VMEM(fin_shape(nb, width), BF16),
        pltpu.VMEM((nb, 4, 4) + tile, BF16),
        pltpu.VMEM((nb, 4, 4) + tile, BF16),
        pltpu.VMEM((3, nb, 4) + tile, BF16),
        pltpu.VMEM((nb, 4) + tile, BF16),
        pltpu.VMEM((3, nb) + tile, BF16),
        pltpu.VMEM((nb,) + tile, BF16),
        pltpu.VMEM((3, nb) + tile, BF16),
        pltpu.VMEM(fin_shape(nb, width), BF16),
    )


def sem_pair(n):
    return (pltpu.SemaphoreType.DMA((n,)), pltpu.SemaphoreType.DMA((n,)))


def widen(
    fa, fb, fc, vec, new_nodes, node_grad, edge_grad,
    new_nodes_o, node_grad_o, edge_grad_o, edge_inner, edge_outer, node_inner, node_outer,
    v0, v1, v2, v3, v4, v5,
    va, vb, vc, vn, vg, ve, wide, in_sem, out_sem,
):
    outs = []

    def load(k, src, dst):
        c = pltpu.make_async_copy(src, dst, in_sem.at[k])
        c.start()
        return c

    def store(k, src, dst):
        c = pltpu.make_async_copy(src, dst, out_sem.at[k])
        c.start()
        outs.append(c)

    c_a = [load(h, fa.at[h], va.at[h]) for h in range(2)]
    c_b = [load(2 + h, fb.at[h], vb.at[h]) for h in range(2)]
    c_c = [load(4 + h, fc.at[h], vc.at[h]) for h in range(2)]
    c_e = [load(7 + k, edge_grad.at[pl.ds(k * 512, 512)], ve.at[pl.ds(k * 512, 512)]) for k in range(4)]
    c_n = load(11, new_nodes, vn)
    c_g = load(12, node_grad, vg)
    k_out = 0
    HALF = NODE // 2

    places = ((node_inner, 0), (node_inner, 512), (node_outer, 0))
    for h in range(2):
        c_a[h].wait()
        for j, (out, first) in enumerate(places):
            rows = pl.ds(j * 512 + h * HALF, HALF)
            wide[rows, :] = va[h, j].reshape(HALF, D).astype(F32)
            store(k_out, wide.at[rows], out.at[pl.ds(first + h * HALF, HALF)])
            k_out += 1
    for h in range(2):
        c_b[h].wait()
        c_c[h].wait()
        for j in range(3):
            rows = pl.ds(1536 + j * 512 + h * HALF, HALF)
            wide[rows, 0:HALF] = vb[h, j].reshape(HALF, HALF).astype(F32)
            wide[rows, HALF:D] = vc[h, j].reshape(HALF, HALF).astype(F32)
            store(k_out, wide.at[rows], edge_inner.at[pl.ds(j * 512 + h * HALF, HALF)])
            k_out += 1
    for h in range(2):
        rows = pl.ds(3072 + h * HALF, HALF)
        for j in range(2):
            wide[rows, j * HALF : (j + 1) * HALF] = vb[h, 3 + j].reshape(HALF, HALF).astype(F32)
        store(k_out, wide.at[rows], edge_outer.at[pl.ds(h * HALF, HALF)])
        k_out += 1
    for k in range(4):
        c_e[k].wait()
        store(k_out, ve.at[pl.ds(k * 512, 512)], edge_grad_o.at[pl.ds(k * 512, 512)])
        k_out += 1
    c_n.wait()
    store(k_out, vn, new_nodes_o)
    c_g.wait()
    store(k_out + 1, vg, node_grad_o)
    for k, out in enumerate((v0, v1, v2, v3, v4, v5)):
        out[...] = vec[k : k + 1, :]
    for c in outs:
        c.wait()


def unpack(outs):
    new_nodes, node_grad, edge_grad, fa, fb, fc, vec = outs
    hbm = pl.BlockSpec(memory_space=pl.ANY)
    vm = pl.BlockSpec(memory_space=pltpu.VMEM)
    shapes = [
        ((NODE, D), BF16), ((NODE, D), BF16), ((EDGE, D), BF16),
        ((3 * D, D), F32), ((D, D), F32), ((2 * D, D), F32), ((D, D), F32),
    ] + [((1, D), F32)] * 6
    scratch = [pltpu.VMEM(fin_shape(*f), BF16) for f in FINS]
    return pl.pallas_call(
        widen,
        out_shape=[jax.ShapeDtypeStruct(s, t) for s, t in shapes],
        in_specs=[hbm] * 3 + [vm] + [hbm] * 3,
        out_specs=[hbm] * 7 + [vm] * 6,
        scratch_shapes=scratch + [
            pltpu.VMEM((NODE, D), BF16), pltpu.VMEM((NODE, D), BF16), pltpu.VMEM((EDGE, D), BF16),
            pltpu.VMEM((7 * D, D), F32),
            pltpu.SemaphoreType.DMA((13,)), pltpu.SemaphoreType.DMA((20,)),
        ],
        compiler_params=pltpu.CompilerParams(vmem_limit_bytes=63 * 2**20),
        name="widen",
    )(fa, fb, fc, vec, new_nodes, node_grad, edge_grad)


def body(
    node_states, edge_states, senders, receivers, live_count, send_rows, node_cotangent,
    edge_inner, edge_inbias, edge_outer, edge_outbias, edge_gain,
    node_inner, node_inbias, node_outer, node_outbias, node_gain,
):
    hbm = pl.BlockSpec(memory_space=pl.ANY)
    vm = pl.BlockSpec(memory_space=pltpu.VMEM)
    sm = pl.BlockSpec(memory_space=pltpu.SMEM)

    def row(v):
        return v.reshape(1, D)

    def v(shape, dtype=BF16):
        return pltpu.VMEM(shape, dtype)

    outs = pl.pallas_call(
        layer,
        out_shape=[
            jax.ShapeDtypeStruct((NODE, D), BF16),
            jax.ShapeDtypeStruct((NODE, D), BF16),
            jax.ShapeDtypeStruct((EDGE, D), BF16),
        ]
        + [jax.ShapeDtypeStruct(fin_shape(*f), BF16) for f in FINS]
        + [jax.ShapeDtypeStruct((8, D), F32)],
        in_specs=[
            hbm, hbm, vm, vm, sm, vm, hbm,
            hbm, vm, hbm, vm, vm, hbm, vm, hbm, vm, vm,
        ],
        out_specs=[hbm] * 7,
        scratch_shapes=[
            v((NODE, D)), v((EDGE, D)), v((NODE, D)),
            v((3 * D, D)), v((D, D)), v((2 * D, D)), v((D, D)),
            v((EDGE, TABLE)), v((TALL, EDGE)), v((EDGE, NODE)),
            v((EDGE, D), F32), v((EDGE, D)), v((EDGE, D)), v((EDGE, 1), F32),
            v((EDGE, D)), v((EDGE, D)), v((3, PART, D), F32),
            v((WIDE, D)), v((NODE, D)), v((WIDE, D)),
            v((8, SLOT, D)), v((8, SLOT, D)), v((8, SLOT, D)), v((8, SLOT, D)),
            v((NODE, PEER)),
            v((NODE, D)), v((NODE, D), F32), v((NODE, D)), v((NODE, D)),
            v((NODE, D), F32), v((D, D), F32),
            v((NODE, D), F32), v((NODE, D), F32), v((NODE, D)), v((NODE, D)), v((NODE, D)),
            v((6, 8, D), F32),
        ]
        + [reduce_bufs(*f) for f in FINS]
        + [
            v((5, 8, D), F32), v((10, 8, D), F32),
            pltpu.SemaphoreType.DMA((7,)), pltpu.SemaphoreType.DMA((11,)),
            pltpu.SemaphoreType.DMA((16,)), pltpu.SemaphoreType.DMA((16,)),
            sem_pair(51), sem_pair(55), sem_pair(51), sem_pair(10),
        ],
        compiler_params=pltpu.CompilerParams(
            collective_id=0, has_side_effects=True, vmem_limit_bytes=63 * 2**20
        ),
        name="layer",
    )(
        node_states, edge_states, senders.reshape(16, LANE), receivers.reshape(16, LANE),
        live_count, send_rows, node_cotangent,
        edge_inner, row(edge_inbias), edge_outer, row(edge_outbias), row(edge_gain),
        node_inner, row(node_inbias), node_outer, row(node_outbias), row(node_gain),
    )
    new_nodes, node_grad, edge_grad, ei, eo, ni, no, *vecs = unpack(outs)
    vecs = [x.reshape(D) for x in vecs]
    return (
        new_nodes, node_grad, edge_grad,
        ei, vecs[0], eo, vecs[1], vecs[2],
        ni, vecs[3], no, vecs[4], vecs[5],
    )


def solution(mesh):
    nodes = P(("lat", "lon"), None)
    flat = P(("lat", "lon"))
    return jax.shard_map(
        body,
        mesh=mesh,
        in_specs=(nodes, nodes, flat, flat, flat, nodes, nodes) + (P(),) * 10,
        out_specs=(nodes, nodes, nodes) + (P(),) * 10,
        check_vma=False,
    )
```
